32 devices in a mesh: sx: 8 (over z, y), sy: 4 (over x, core).
Axes of the slice: x: 2, y: 2, z: 4, core: 2. Of those that a mesh axis runs over, the one named last changes fastest.
Arguments:
- rhs: float32 [6144, 8192], P('sx', 'sy')
- sigma: float32 [6144, 8192], P('sx', 'sy'), may hold values from 0.05 to 2
- tile_list: int32 [65536], P(('sx', 'sy')), may hold values from 0 to 12287, as said below
- tile_owner: int32 [65536, 1], P(('sx', 'sy')), may hold values from 0 to 31, as said below
- schur_blocks: bfloat16 [32, 128, 128], P(('sx', 'sy')), as said below
Outputs:
- corrected: float32 [6144, 8192], P('sx', 'sy')
- iface_residual: float32 [65536, 128], P(('sx', 'sy'))
- iface_direction: float32 [65536, 128], P(('sx', 'sy'))
The draws below stay inside these ranges and needn't reach their ends.
Inputs may be any that keep to these rules, and one draw needn't show every extreme that they name: `tile_owner`: within the 2048 tiles of one subdomain no owner appears more than 128 times. `tile_list`: every listed run touches its block's rim: it lies in the block's first or last row, or is the first or last run of its row. Runs may repeat. `schur_blocks`: each block is symmetric.
All inputs are finite; a program needn't handle non-finite values.
Results may differ from the reference program's by a relative error of at most 0.012.
Values may be sent and summed in bfloat16 or wider, within the bound.
A program may use at most 128 MiB of HBM per device.

```python
import math
import jax
import jax.numpy as jnp
from jax import lax

CR = 768
CC = 2048
TW = 128
TPD = 2048
NROW = 6144
NCOL = 8192
TILES = 65536
N_SX = 8
N_SY = 4


def draw_rhs(key, part):
    key_two = jax.random.fold_in(jax.random.fold_in(key, 11), 1)
    rowpos = jnp.arange(NROW, dtype=jnp.float32) / NROW
    colpos = jnp.arange(NCOL, dtype=jnp.float32) / NCOL
    scale = (1.0 + rowpos[:, None]) * (1.0 + colpos[None, :])
    return jax.random.normal(key_two, (NROW, NCOL), jnp.float32) * scale


def draw_tile_list(key, part):
    runs = CC // TW
    count = N_SX * N_SY
    rim_total = 2 * runs + 2 * (CR - 2)
    pick = jax.random.randint(jax.random.fold_in(key, 37), (count, TPD), 0, rim_total, jnp.int32)
    bottom = (CR - 1) * runs + (pick - runs)
    side_pos = pick - 2 * runs
    row_side = 1 + side_pos // 2
    edge = row_side * runs + side_pos % 2 * (runs - 1)
    chosen = jnp.where(pick < runs, pick, jnp.where(pick < 2 * runs, bottom, edge))
    chosen = chosen.at[:, 0].set(0).at[:, 1].set(CR * runs - 1)
    return chosen.astype(jnp.int32).reshape(count * TPD)


def owner_order(key):
    count = N_SX * N_SY
    return jax.random.permutation(jax.random.fold_in(key, 71), count).astype(jnp.int32)


def draw_tile_owner(key, part):
    count = N_SX * N_SY
    half_count = count // 2
    capacity = 2 * TPD // count
    order = owner_order(key)
    base_key = jax.random.fold_in(key, 73)
    denom = 2 * (N_SX - 1) * (N_SY - 1)

    def one_device(device):
        row_index = device // N_SY
        col_index = device % N_SY
        start = 1 + (row_index * (N_SY - 1) + col_index * (N_SX - 1)) * (half_count - 1) // denom
        sub_key = jax.random.fold_in(base_key, device)
        key_one, key_two = jax.random.split(sub_key)
        ranks = start + jnp.arange(half_count * capacity, dtype=jnp.int32) // capacity
        picked = jax.random.permutation(key_one, ranks)[:TPD - capacity]
        pool = jnp.concatenate([jnp.zeros((capacity,), jnp.int32), picked.astype(jnp.int32)])
        pool = jax.random.permutation(key_two, pool)
        return order[pool]
    owners = jax.vmap(one_device)(jnp.arange(count, dtype=jnp.int32))
    return owners.astype(jnp.int32).reshape(count * TPD, 1)


def draw_schur_blocks(key, part):
    key_one, key_two = jax.random.split(jax.random.fold_in(key, 23))
    count = N_SX * N_SY
    order = owner_order(key)
    rank = jnp.zeros((count,), jnp.int32).at[order].set(jnp.arange(count, dtype=jnp.int32))
    level = 2.0 * jnp.power(4.0, rank.astype(jnp.float32) / (count - 1))
    raw = jax.random.uniform(key_one, (count, TW, TW), jnp.float32, -0.25, 0.25)
    diag = jax.random.uniform(key_two, (count, TW), jnp.float32, 3.5, 5.0)
    sym = 0.5 * (raw + jnp.swapaxes(raw, 1, 2))
    eye = jnp.eye(TW, dtype=jnp.float32)
    full = sym * (1.0 - eye)[None] + eye[None] * diag[:, :, None]
    full = full * (0.25 * level)[:, None, None]
    return full.astype(jnp.bfloat16)


def level_of(key, shape, pieces, low, high):
    factor_of = 1.0
    for position, blocks in pieces:
        heights = jax.random.uniform(jax.random.fold_in(jax.random.fold_in(key, 6), position), (blocks,), jnp.float32, low / len(pieces), high / len(pieces))
        factor_of = factor_of * jnp.repeat(jnp.exp(heights), shape[position] // blocks).reshape((-1,) + (1,) * (len(shape) - 1 - position))
    return factor_of


def setup_inputs(seed: int = 0) -> dict:
    arg_keys = jax.random.split(jax.random.key(seed), 6)
    return {
        "rhs": draw_rhs(jax.random.fold_in(arg_keys[5], 71), 0),
        "sigma": jnp.clip(jnp.exp(math.log(2.0) - 3.6888794 * jax.random.uniform(arg_keys[1], (NROW, NCOL), jnp.float32) ** level_of(arg_keys[1], (NROW, NCOL), ((0, 8), (1, 4)), -0.2, 0.2)), 0.05, 2.0),
        "tile_list": draw_tile_list(jax.random.fold_in(arg_keys[5], 71), 0),
        "tile_owner": draw_tile_owner(jax.random.fold_in(arg_keys[5], 71), 0),
        "schur_blocks": draw_schur_blocks(jax.random.fold_in(arg_keys[5], 71), 0),
    }


def apply_op(field, sigma):
    padded = jnp.pad(field, 1)
    beside = padded[2:, 1:-1] + padded[:-2, 1:-1] + padded[1:-1, 2:] + padded[1:-1, :-2]
    return (4.0 + sigma) * field - beside


def to_blocks(field):
    return field.reshape(N_SX, CR, N_SY, CC).transpose(0, 2, 1, 3).reshape(N_SX * N_SY, CR * CC // TW, TW)


def reference(rhs, sigma, tile_list, tile_owner, schur_blocks):
    dinv = 1.0 / (4.0 + sigma)
    first = 0.6111111 * dinv * rhs
    second = first + 2.75 * dinv * (rhs - apply_op(first, sigma))
    field_res = rhs - apply_op(second, sigma)
    lists = tile_list.reshape(N_SX * N_SY, TPD)
    owners = tile_owner.reshape(N_SX * N_SY, TPD)
    r_tiles = jax.vmap(lambda blk, idx: blk[idx])(to_blocks(field_res), lists)

    def one_source(pair):
        tiles, own = pair
        mats = schur_blocks[own].astype(jnp.float32)
        half = lax.optimization_barrier(tiles.astype(jnp.bfloat16)).astype(jnp.float32)
        prod = jnp.einsum('tc,tcn->tn', half, mats)
        return lax.optimization_barrier(prod.astype(jnp.bfloat16)).astype(jnp.float32)

    q_tiles = lax.map(one_source, (r_tiles, owners))
    rr_old = jnp.sum(r_tiles * r_tiles)
    pq_sum = jnp.sum(r_tiles * q_tiles)
    alpha = rr_old / pq_sum
    iface_residual = r_tiles - alpha * q_tiles
    rr_new = jnp.sum(iface_residual * iface_residual)
    iface_direction = iface_residual + (rr_new / rr_old) * r_tiles
    added = jax.vmap(lambda blk, idx, val: blk.at[idx].add(val))(to_blocks(second), lists, alpha * r_tiles)
    corrected = added.reshape(N_SX, N_SY, CR, CC).transpose(0, 2, 1, 3).reshape(NROW, NCOL)
    return corrected, iface_residual.reshape(TILES, TW), iface_direction.reshape(TILES, TW)
```

```python
import functools

import jax
import jax.numpy as jnp
from jax import lax
from jax.experimental import pallas as pl
from jax.experimental.pallas import tpu as pltpu
from jax.sharding import PartitionSpec as P

MESH = pl.DeviceIdType.MESH
W1 = 0.6111111
W2 = 2.75
CC = W1 + W2 * (1.0 - W1)
LANES = 128
F32 = jnp.float32
BF16 = jnp.bfloat16


def halo_sum(ref, row, col, rows, width):
    if rows == 8:
        ref = ref.at[pl.ds(row, 24)]
        row = 0
    wide = ref[row + 8 : row + 8 + rows, col : col + width + 2 * LANES]
    total = width + 2 * LANES
    left = pltpu.roll(wide, 1, 1)[:, LANES : LANES + width]
    right = pltpu.roll(wide, total - 1, 1)[:, LANES : LANES + width]
    up = ref[row + 7 : row + 7 + rows, col + LANES : col + LANES + width]
    down = ref[row + 9 : row + 9 + rows, col + LANES : col + LANES + width]
    return (left + right) + (up + down)


def spans(c0, c1, step):
    return [(c, min(step, c1 - c)) for c in range(c0, c1, step)]


def front_kernel(nsx, nsy, rhs_h, sig_h, idx_ref, own_ref, sch_ref,
                 sp, cr, r_out, q_out, sums_out,
                 rhs_v, d_v, fp, rb, blocks, row_s, row_r, col_s, col_r, sum_buf,
                 in_sem, hs_sem, hr_sem, ag_r, ss_z, ss_y, ss_x, ss_c, sum_s, sum_r):
    rows, cols = rhs_v.shape
    tiles = r_out.shape[0]
    runs = cols // LANES
    nz, nx = nsx // 2, nsy // 2
    n = nsx * nsy
    sx = lax.axis_index("sx")
    sy = lax.axis_index("sy")
    me = sx * nsy + sy
    z, y = lax.div(sx, 2), lax.rem(sx, 2)
    x, c = lax.div(sy, 2), lax.rem(sy, 2)

    left, right = (0, 2 * LANES), (cols - 2 * LANES, cols)
    regions = [(0, rows) + left, (0, rows) + right,
               (0, 16, left[1], right[0]), (rows - 16, rows, left[1], right[0])]
    chunks = 4
    step = (rows - 32) // chunks // 8 * 8
    cuts = [16 + step * i for i in range(chunks)] + [rows - 16]
    for i in range(chunks):
        regions.append((cuts[i], cuts[i + 1], left[1], right[0]))
    loads = []
    for i, (r0, r1, c0, c1) in enumerate(regions):
        pair = []
        for k, (src, dst) in enumerate(((rhs_h, rhs_v), (sig_h, d_v))):
            cp = pltpu.make_async_copy(src.at[r0:r1, c0:c1], dst.at[r0:r1, c0:c1], in_sem.at[k, i])
            cp.start()
            pair.append(cp)
        loads.append(pair)

    barrier = pltpu.get_barrier_semaphore()

    @pl.loop(1, n)
    def _(k):
        o = lax.rem(me + k, n)
        pl.semaphore_signal(barrier, inc=1, device_id=(lax.div(o, nsy), lax.rem(o, nsy)),
                            device_id_type=MESH)

    blocks[c, (2 * z + y) * nx + x] = sch_ref[...]
    pl.semaphore_wait(barrier, n - 1)

    half = LANES // 2

    def piece(h, zz, yy, xx, cc, dev, sem):
        pair = (2 * zz + yy) * nx + xx
        ref = blocks.at[cc, pair, pl.ds(h * half, half), :]
        dz, dy, dx, dc = dev
        return pltpu.make_async_remote_copy(
            ref, ref, sem, ag_r.at[h, 2 * pair + cc],
            device_id=(2 * dz + dy, 2 * dx + dc), device_id_type=MESH)

    sends = []

    def send(*args):
        cp = piece(*args)
        cp.start()
        sends.append(cp)

    def arrived(h, zz, yy, xx, cc):
        piece(h, zz, yy, xx, cc, (z, y, x, 1 - c), ss_c.at[0, 0, 0, 0]).wait_recv()

    zs = [lax.rem(z + k, nz) for k in range(nz)]
    ys = [y, 1 - y]
    xs = [lax.rem(x + k, nx) for k in range(nx)]

    def to_core(h, i, j, k):
        send(h, zs[i], ys[j], xs[k], c, (z, y, x, 1 - c), ss_c.at[h, i, j, k])

    for h in range(2):
        for i in range(1, nz):
            send(h, z, y, x, c, (zs[i], y, x, c), ss_z.at[h, i])

    def ag_first(i):
        for h in range(2):
            if i:
                arrived(h, zs[i], y, x, c)
            if h == 0:
                send(0, zs[i], y, x, c, (z, 1 - y, x, c), ss_y.at[0, i, 0])
            for k in range(1, nx):
                send(h, zs[i], y, x, c, (z, y, xs[k], c), ss_x.at[h, i, 0, k])
            if h == 1:
                send(1, zs[i], y, x, c, (z, 1 - y, x, c), ss_y.at[1, i, 0])
            to_core(h, i, 0, 0)

    def ag_second(i):
        arrived(0, zs[i], 1 - y, x, c)
        for k in range(1, nx):
            send(0, zs[i], 1 - y, x, c, (z, y, xs[k], c), ss_x.at[0, i, 1, k])
        to_core(0, i, 1, 0)
        for k in range(1, nx):
            arrived(1, zs[i], y, xs[k], c)
            send(1, zs[i], y, xs[k], c, (z, 1 - y, x, c), ss_y.at[1, i, k])
            to_core(1, i, 0, k)

    def ag_third(i):
        for k in range(1, nx):
            arrived(0, zs[i], y, xs[k], c)
            to_core(0, i, 0, k)
            arrived(0, zs[i], 1 - y, xs[k], c)
            to_core(0, i, 1, k)
        for k in range(nx):
            arrived(1, zs[i], 1 - y, xs[k], c)
            to_core(1, i, 1, k)

    def ag_last():
        for h in range(2):
            for i in range(nz):
                for j in range(2):
                    for k in range(nx):
                        arrived(h, zs[i], ys[j], xs[k], 1 - c)

    def do_first(r0, r1, c0, c1):
        @pl.loop(r0 // 8, r1 // 8)
        def _(t):
            r = pl.multiple_of(t * 8, 8)
            for col, w in spans(c0, c1, 512):
                rhs = rhs_v[pl.ds(r, 8), col : col + w]
                dinv = 1.0 / (4.0 + d_v[pl.ds(r, 8), col : col + w])
                d_v[pl.ds(r, 8), col : col + w] = dinv
                fp[pl.ds(r + 8, 8), col + LANES : col + LANES + w] = W1 * dinv * rhs

    def do_second(r0, r1, c0, c1):
        @pl.loop(r0 // 8, r1 // 8)
        def _(t):
            r = pl.multiple_of(t * 8, 8)
            for col, w in spans(c0, c1, 1024):
                beside = halo_sum(fp, r, col, 8, w)
                rhs = rhs_v[pl.ds(r, 8), col : col + w]
                dinv = d_v[pl.ds(r, 8), col : col + w]
                sp[pl.ds(r + 8, 8), col + LANES : col + LANES + w] = dinv * (CC * rhs + W2 * beside)

    lane = lax.broadcasted_iota(jnp.int32, (8, LANES), 1)
    up_dev = (lax.rem(sx + nsx - 1, nsx), sy)
    down_dev = (lax.rem(sx + 1, nsx), sy)
    left_dev = (sx, lax.rem(sy + nsy - 1, nsy))
    right_dev = (sx, lax.rem(sy + 1, nsy))

    def halo_copies(ph):
        out = []
        for k, dev in enumerate((up_dev, down_dev)):
            out.append(pltpu.make_async_remote_copy(
                row_s.at[ph, k], row_r.at[ph, k], hs_sem.at[ph, k], hr_sem.at[ph, k],
                device_id=dev, device_id_type=MESH))
        for k, dev in enumerate((left_dev, right_dev)):
            out.append(pltpu.make_async_remote_copy(
                col_s.at[ph, k], col_r.at[ph, k], hs_sem.at[ph, 2 + k], hr_sem.at[ph, 2 + k],
                device_id=dev, device_id_type=MESH))
        return out

    def halo_send(ph, ref):
        row_s[ph, 0] = ref[8:9, LANES : LANES + cols]
        row_s[ph, 1] = ref[rows + 7 : rows + 8, LANES : LANES + cols]
        one = jnp.zeros((8, LANES), F32)
        two = jnp.zeros((8, LANES), F32)
        for i in range(rows // 8):
            a = ref[8 + 8 * i : 16 + 8 * i, LANES : 2 * LANES]
            b = ref[8 + 8 * i : 16 + 8 * i, cols : cols + LANES]
            one = jnp.where(lane == i, a[:, 0:1], one)
            two = jnp.where(lane == i, b[:, LANES - 1 : LANES], two)
        col_s[ph, 0] = one
        col_s[ph, 1] = two
        cps = halo_copies(ph)
        for cp in cps:
            cp.start()
        return cps

    def halo_take(ph, ref, cps):
        for cp in cps:
            cp.wait_recv()
        zero_row = jnp.zeros((1, cols), F32)
        ref[7:8, LANES : LANES + cols] = jnp.where(sx > 0, row_r[ph, 1], zero_row)
        ref[rows + 8 : rows + 9, LANES : LANES + cols] = jnp.where(sx < nsx - 1, row_r[ph, 0], zero_row)
        zero = jnp.zeros((8, LANES), F32)
        from_left = jnp.where(sy > 0, col_r[ph, 1], zero)
        from_right = jnp.where(sy < nsy - 1, col_r[ph, 0], zero)
        for i in range(rows // 8):
            ref[8 + 8 * i : 16 + 8 * i, 0:LANES] = jnp.broadcast_to(from_left[:, i : i + 1], (8, LANES))
            ref[8 + 8 * i : 16 + 8 * i, cols + LANES : cols + 2 * LANES] = jnp.broadcast_to(
                from_right[:, i : i + 1], (8, LANES))

    for i in range(4):
        for cp in loads[i]:
            cp.wait()
        do_first(*regions[i])
    cps0 = halo_send(0, fp)
    ag_first(0)
    for cp in loads[4]:
        cp.wait()
    do_first(*regions[4])
    for i in range(1, nz):
        ag_first(i)
    halo_take(0, fp, cps0)
    do_second(0, rows, *left)
    do_second(0, rows, *right)
    do_second(0, 8, LANES, cols - LANES)
    do_second(rows - 8, rows, LANES, cols - LANES)
    cps1 = halo_send(1, sp)
    for i in range(nz):
        ag_second(i)
    for i in range(5, 4 + chunks):
        for cp in loads[i]:
            cp.wait()
        do_first(*regions[i])
    for i in range(nz):
        ag_third(i)

    index = idx_ref[...]
    owner = own_ref[...]
    trow = lax.div(index, runs)
    tcol = index - trow * runs
    rid = jnp.where(tcol == 0, trow, jnp.where(tcol == runs - 1, rows + trow, jnp.where(
        trow == 0, 2 * rows + tcol, 2 * rows + runs + tcol)))
    ra = lax.shift_right_logical(rid, 7)
    rbm = rid & (LANES - 1)
    pr = lax.shift_right_logical(owner, 1)
    par = owner & 1
    nblk = tiles // LANES
    stack = jnp.concatenate([v.astype(F32) for v in (ra, rbm, pr, par)]
                            + [jnp.zeros((LANES - 4 * nblk, LANES), F32)], axis=0)
    numbers = stack.T

    halo_take(1, sp, cps1)

    def rim(row, col, nrows, width):
        return ((1.0 - CC) * rhs_v[pl.ds(row, nrows), col : col + width]
                - W2 * halo_sum(fp, row, col, nrows, width) + halo_sum(sp, row, col, nrows, width))

    def put(at, nrows, value):
        cr[pl.ds(at, nrows), :] = value

    @pl.loop(0, rows // 16)
    def _(t):
        for u in range(2):
            r = pl.multiple_of(t * 16 + u * 8, 8)
            put(r, 8, rim(r, 0, 8, LANES))
            put(r + rows, 8, rim(r, cols - LANES, 8, LANES))

    cr[2 * rows :, :] = jnp.zeros((cr.shape[0] - 2 * rows, LANES), F32)
    top = rim(0, 0, 1, cols)
    bottom = rim(rows - 1, 0, 1, cols)
    for k in range(runs):
        put(2 * rows + k, 1, top[:, LANES * k : LANES * k + LANES])
        put(2 * rows + runs + k, 1, bottom[:, LANES * k : LANES * k + LANES])

    nk = cr.shape[0] // LANES

    @pl.loop(0, nk)
    def _(t):
        at = pl.multiple_of(t * LANES, LANES)
        v = cr[pl.ds(at, LANES), :]
        hi = v.astype(BF16)
        rb[pl.ds(at, LANES), 0:LANES] = hi
        rb[pl.ds(at, LANES), LANES:] = (v - hi.astype(F32)).astype(BF16)

    ag_last()
    m = 4
    lanes_m = lax.broadcasted_iota(jnp.int32, (m * LANES, LANES), 1).astype(F32)
    zero_b = jnp.zeros((m * LANES, LANES), BF16)
    count = jnp.zeros((LANES, LANES), F32)
    rr = jnp.zeros((8, LANES), F32)
    pq = jnp.zeros((8, LANES), F32)
    qq = jnp.zeros((8, LANES), F32)

    def spread(kind, g):
        return jnp.concatenate([
            jnp.broadcast_to(numbers[:, kind * nblk + g * m + u : kind * nblk + g * m + u + 1],
                             (LANES, LANES)) for u in range(m)], axis=0)

    def fold(v):
        return jnp.sum(v.reshape(-1, 8, LANES), axis=0)

    npair = blocks.shape[1]
    gp = min(npair, 16)
    for g in range(nblk // m):
        at = g * m * LANES
        a32 = spread(0, g)
        a16 = a32.astype(BF16)
        base = jnp.where(spread(1, g) == lanes_m, 1.0, 0.0).astype(BF16)
        aone = jnp.where(a32 == lanes_m, 1.0, 0.0).astype(BF16)
        count += lax.dot_general(base, aone, (((0,), (0,)), ((), ())), preferred_element_type=F32)
        hot = jnp.concatenate([jnp.where(a16 == k, base, zero_b) for k in range(nk)], axis=1)
        both = jnp.dot(hot, rb[...], preferred_element_type=F32)
        r = both[:, :LANES] + both[:, LANES:]
        p = both[:, :LANES].astype(BF16)
        r_out[at : at + m * LANES, :] = r
        p16 = spread(2, g).astype(BF16)

        def pairs(k0, acc):
            masked = jnp.concatenate(
                [jnp.where(p16 == (k0 + k if isinstance(k0, int) else (k0 + k).astype(BF16)), p, zero_b)
                 for k in range(gp)], axis=1)
            mats = jnp.concatenate([blocks[0, pl.ds(k0, gp)].reshape(gp * LANES, LANES),
                                    blocks[1, pl.ds(k0, gp)].reshape(gp * LANES, LANES)], axis=1)
            return acc + jnp.dot(masked, mats, preferred_element_type=F32)

        acc = jnp.zeros((m * LANES, 2 * LANES), F32)
        if npair == gp:
            acc = pairs(0, acc)
        else:
            acc = lax.fori_loop(0, npair // gp, lambda s, v: pairs(s * gp, v), acc)
        qb = jnp.where(spread(3, g) > 0.5, acc[:, LANES:], acc[:, :LANES]).astype(BF16)
        q_out[at : at + m * LANES, :] = qb
        q = qb.astype(F32)
        rr += fold(r * r)
        pq += fold(r * q)
        qq += fold(q * q)

    part = jnp.concatenate([jnp.sum(v, axis=0, keepdims=True) for v in (rr, pq, qq)]
                           + [jnp.zeros((5, LANES), F32)], axis=0)
    sum_buf[me] = part

    def sum_copy(slot, k):
        o = lax.rem(me + k, n)
        return pltpu.make_async_remote_copy(
            sum_buf.at[slot], sum_buf.at[slot], sum_s.at[k], sum_r.at[slot],
            device_id=(lax.div(o, nsy), lax.rem(o, nsy)), device_id_type=MESH)

    @pl.loop(1, n)
    def _(k):
        sum_copy(me, k).start()

    do_second(8, rows - 8, LANES, cols - LANES)
    for a in range(nk):
        at = a * LANES
        cr[at : at + LANES, :] = cr[at : at + LANES, :] * count[:, a : a + 1]

    for cp in cps0 + cps1:
        cp.wait_send()
    for cp in sends:
        cp.wait_send()

    @pl.loop(1, n)
    def _(k):
        sum_copy(me, k).wait_send()
        sum_copy(lax.rem(me + k, n), k).wait_recv()

    sums_out[...] = jnp.sum(sum_buf[...], axis=0)


def back_kernel(sp, cr, r_ref, q_ref, sums, out, res, direc,
                left, right, top, bottom, res_v, dir_v, sem):
    rows, cols = out.shape
    tiles = r_ref.shape[0]
    runs = cols // LANES
    inner = pltpu.make_async_copy(
        sp.at[16 : rows, 2 * LANES : cols],
        out.at[8 : rows - 8, LANES : cols - LANES], sem.at[0])
    inner.start()
    copies = [inner]
    total = jnp.sum(sums[...], axis=1, keepdims=True)
    rr, pq, qq = total[0:1], total[1:2], total[2:3]
    alpha = rr / pq
    beta = (rr - 2.0 * alpha * pq + alpha * alpha * qq) / rr

    nch = 4
    size = tiles // nch
    for k in range(nch):
        sl = slice(k * size, (k + 1) * size)

        @pl.loop(0, size // 64)
        def _(t, k=k):
            at = pl.multiple_of(k * size + t * 64, 64)
            r = r_ref[pl.ds(at, 64), :]
            v = r - alpha * q_ref[pl.ds(at, 64), :].astype(F32)
            res_v[pl.ds(at, 64), :] = v
            dir_v[pl.ds(at, 64), :] = v + beta * r

        for src, dst, i in ((res_v, res, 1 + k), (dir_v, direc, 1 + nch + k)):
            cp = pltpu.make_async_copy(src.at[sl], dst.at[sl], sem.at[i])
            cp.start()
            copies.append(cp)

    @pl.loop(0, rows // 64)
    def _(t):
        at = pl.multiple_of(t * 64, 64)
        left[pl.ds(at, 64), :] = sp[pl.ds(at + 8, 64), LANES : 2 * LANES] + alpha * cr[pl.ds(at, 64), :]
        right[pl.ds(at, 64), :] = (sp[pl.ds(at + 8, 64), cols : cols + LANES]
                                   + alpha * cr[pl.ds(at + rows, 64), :])

    top[...] = sp[8:16, 2 * LANES : cols]
    bottom[...] = sp[rows : rows + 8, 2 * LANES : cols]
    for k in range(1, runs - 1):
        sl = slice((k - 1) * LANES, k * LANES)
        top[0:1, sl] = top[0:1, sl] + alpha * cr[2 * rows + k : 2 * rows + k + 1, :]
        bottom[7:8, sl] = bottom[7:8, sl] + alpha * cr[2 * rows + runs + k : 2 * rows + runs + k + 1, :]
    i = 1 + 2 * nch
    for src, dst in ((left, out.at[:, 0:LANES]), (right, out.at[:, cols - LANES : cols]),
                     (top, out.at[0:8, LANES : cols - LANES]),
                     (bottom, out.at[rows - 8 : rows, LANES : cols - LANES])):
        cp = pltpu.make_async_copy(src, dst, sem.at[i])
        cp.start()
        copies.append(cp)
        i += 1
    for cp in copies:
        cp.wait()


def per_device(nsx, nsy, rhs, sigma, tile_list, tile_owner, schur_blocks):
    rows, cols = rhs.shape
    tiles = tile_list.shape[0]
    n = nsx * nsy
    nz, nx = nsx // 2, nsy // 2
    nk = -(-(2 * rows + 2 * (cols // LANES)) // LANES)
    vm = pl.BlockSpec(memory_space=pltpu.VMEM)
    hbm = pl.BlockSpec(memory_space=pl.ANY)
    dma = pltpu.SemaphoreType.DMA
    padded = (rows + 16, cols + 2 * LANES)
    kept = pltpu.VMEM
    sp, cr, r, q, sums = pl.pallas_call(
        functools.partial(front_kernel, nsx, nsy),
        out_shape=[kept(padded, F32), kept((nk * LANES, LANES), F32), kept((tiles, LANES), F32),
                   kept((tiles, LANES), BF16), kept((8, LANES), F32)],
        in_specs=[hbm, hbm, vm, vm, vm],
        out_specs=[vm] * 5,
        scratch_shapes=[
            pltpu.VMEM((rows, cols), F32), pltpu.VMEM((rows, cols), F32), pltpu.VMEM(padded, F32),
            pltpu.VMEM((nk * LANES, 2 * LANES), BF16), pltpu.VMEM((2, n // 2, LANES, LANES), BF16),
            pltpu.VMEM((2, 2, 1, cols), F32), pltpu.VMEM((2, 2, 1, cols), F32),
            pltpu.VMEM((2, 2, 8, LANES), F32), pltpu.VMEM((2, 2, 8, LANES), F32),
            pltpu.VMEM((n, 8, LANES), F32),
            dma((2, 8)), dma((2, 4)), dma((2, 4)), dma((2, n)), dma((2, nz)), dma((2, nz, nx)),
            dma((2, nz, 2, nx)), dma((2, nz, 2, nx)), dma((n,)), dma((n,)),
        ],
        compiler_params=pltpu.CompilerParams(
            collective_id=0, has_side_effects=True, vmem_limit_bytes=44 * 2**20),
        name="front",
    )(rhs, sigma, tile_list.reshape(-1, LANES), tile_owner.reshape(-1, LANES),
      schur_blocks.reshape(LANES, LANES))
    nch = 4
    return pl.pallas_call(
        back_kernel,
        out_shape=[jax.ShapeDtypeStruct((rows, cols), F32), jax.ShapeDtypeStruct((tiles, LANES), F32),
                   jax.ShapeDtypeStruct((tiles, LANES), F32)],
        in_specs=[vm] * 5,
        out_specs=[hbm] * 3,
        scratch_shapes=[
            pltpu.VMEM((rows, LANES), F32), pltpu.VMEM((rows, LANES), F32),
            pltpu.VMEM((8, cols - 2 * LANES), F32), pltpu.VMEM((8, cols - 2 * LANES), F32),
            pltpu.VMEM((tiles, LANES), F32), pltpu.VMEM((tiles, LANES), F32),
            dma((1 + 2 * nch + 4,)),
        ],
        compiler_params=pltpu.CompilerParams(vmem_limit_bytes=16 * 2**20),
        name="back",
    )(sp, cr, r, q, sums)


def solution(mesh):
    nsx, nsy = mesh.shape["sx"], mesh.shape["sy"]
    in_specs = (
        P("sx", "sy"),
        P("sx", "sy"),
        P(("sx", "sy")),
        P(("sx", "sy"), None),
        P(("sx", "sy"), None, None),
    )
    out_specs = (P("sx", "sy"), P(("sx", "sy"), None), P(("sx", "sy"), None))

    def body(*args):
        return tuple(per_device(nsx, nsy, *args))

    return jax.shard_map(body, mesh=mesh, in_specs=in_specs, out_specs=out_specs, check_vma=False)
```

```python
import functools

import jax
import jax.numpy as jnp
from jax import lax
from jax.experimental import pallas as pl
from jax.experimental.pallas import tpu as pltpu
from jax.sharding import PartitionSpec as P

MESH = pl.DeviceIdType.MESH
W1 = 0.6111111
W2 = 2.75
CC = W1 + W2 * (1.0 - W1)
LANES = 128
F32 = jnp.float32
BF16 = jnp.bfloat16


def halo_sum(ref, row, col, rows, width):
    if not isinstance(row, int):
        ref = ref.at[pl.ds(row, rows + 16)]
        row = 0
    wide = ref[row + 8 : row + 8 + rows, col : col + width + 2 * LANES]
    total = width + 2 * LANES
    left = pltpu.roll(wide, 1, 1)[:, LANES : LANES + width]
    right = pltpu.roll(wide, total - 1, 1)[:, LANES : LANES + width]
    up = ref[row + 7 : row + 7 + rows, col + LANES : col + LANES + width]
    down = ref[row + 9 : row + 9 + rows, col + LANES : col + LANES + width]
    return (left + right) + (up + down)


def front_kernel(nsx, nsy, rhs_h, sig_h, idx_ref, own_ref, sch_ref,
                 sp, cr, r_out, q_out, sums_out,
                 rhs_v, d_v, fp, rb, blocks, idx_v, own_v, p_v, row_s, row_r, col_s, col_r, sum_buf,
                 in_sem, small_sem, hs_sem, hr_sem, ag_r, ss_z, ss_y, ss_x, ss_c, sum_s, sum_r):
    rows, cols = rhs_v.shape
    tiles = r_out.shape[0]
    runs = cols // LANES
    nz, nx = nsx // 2, nsy // 2
    n = nsx * nsy
    sx = lax.axis_index("sx")
    sy = lax.axis_index("sy")
    me = sx * nsy + sy
    z, y = lax.div(sx, 2), lax.rem(sx, 2)
    x, c = lax.div(sy, 2), lax.rem(sy, 2)

    left, right = (0, 2 * LANES), (cols - 2 * LANES, cols)
    regions = [(0, rows) + left, (0, rows) + right,
               (0, 16, left[1], right[0]), (rows - 16, rows, left[1], right[0])]
    chunks = 4
    step = (rows - 32) // chunks // 16 * 16
    cuts = [16 + step * i for i in range(chunks)] + [rows - 16]
    for i in range(chunks):
        regions.append((cuts[i], cuts[i + 1], left[1], right[0]))
    loads = []
    for i, (r0, r1, c0, c1) in enumerate(regions):
        pair = []
        for k, (src, dst) in enumerate(((rhs_h, rhs_v), (sig_h, d_v))):
            cp = pltpu.make_async_copy(src.at[r0:r1, c0:c1], dst.at[r0:r1, c0:c1], in_sem.at[k, i])
            cp.start()
            pair.append(cp)
        loads.append(pair)

    barrier = pltpu.get_barrier_semaphore()

    @pl.loop(1, n)
    def _(k):
        o = lax.rem(me + k, n)
        pl.semaphore_signal(barrier, inc=1, device_id=(lax.div(o, nsy), lax.rem(o, nsy)),
                            device_id_type=MESH)

    small = [pltpu.make_async_copy(src, dst, small_sem.at[i]) for i, (src, dst) in enumerate((
        (sch_ref, blocks.at[c, (2 * z + y) * nx + x]), (idx_ref, idx_v), (own_ref, own_v)))]
    for cp in small:
        cp.start()

    half = LANES // 2

    def piece(h, zz, yy, xx, cc, dev, sem):
        pair = (2 * zz + yy) * nx + xx
        ref = blocks.at[cc, pair, pl.ds(h * half, half), :]
        dz, dy, dx, dc = dev
        return pltpu.make_async_remote_copy(
            ref, ref, sem, ag_r.at[h, 2 * pair + cc],
            device_id=(2 * dz + dy, 2 * dx + dc), device_id_type=MESH)

    sends = []

    def send(*args):
        cp = piece(*args)
        cp.start()
        sends.append(cp)

    def arrived(h, zz, yy, xx, cc):
        piece(h, zz, yy, xx, cc, (z, y, x, 1 - c), ss_c.at[0, 0, 0, 0]).wait_recv()

    zs = [lax.rem(z + k, nz) for k in range(nz)]
    ys = [y, 1 - y]
    xs = [lax.rem(x + k, nx) for k in range(nx)]

    def to_core(h, i, j, k):
        send(h, zs[i], ys[j], xs[k], c, (z, y, x, 1 - c), ss_c.at[h, i, j, k])

    def ag_first(i):
        for h in range(2):
            if i:
                arrived(h, zs[i], y, x, c)
            if h == 0:
                send(0, zs[i], y, x, c, (z, 1 - y, x, c), ss_y.at[0, i, 0])
            for k in range(1, nx):
                send(h, zs[i], y, x, c, (z, y, xs[k], c), ss_x.at[h, i, 0, k])
            if h == 1:
                send(1, zs[i], y, x, c, (z, 1 - y, x, c), ss_y.at[1, i, 0])
            to_core(h, i, 0, 0)

    def ag_second(i):
        arrived(0, zs[i], 1 - y, x, c)
        for k in range(1, nx):
            send(0, zs[i], 1 - y, x, c, (z, y, xs[k], c), ss_x.at[0, i, 1, k])
        to_core(0, i, 1, 0)
        for k in range(1, nx):
            arrived(1, zs[i], y, xs[k], c)
            send(1, zs[i], y, xs[k], c, (z, 1 - y, x, c), ss_y.at[1, i, k])
            to_core(1, i, 0, k)

    def ag_third(i):
        for k in range(1, nx):
            arrived(0, zs[i], y, xs[k], c)
            to_core(0, i, 0, k)
            arrived(0, zs[i], 1 - y, xs[k], c)
            to_core(0, i, 1, k)
        for k in range(nx):
            arrived(1, zs[i], 1 - y, xs[k], c)
            to_core(1, i, 1, k)

    def ag_last():
        for h in range(2):
            for i in range(nz):
                for j in range(2):
                    for k in range(nx):
                        arrived(h, zs[i], ys[j], xs[k], 1 - c)

    def do_first(r0, r1, c0, c1, b):
        w = c1 - c0

        @pl.loop(0, (r1 - r0) // b)
        def _(t):
            r = pl.multiple_of(r0 + t * b, 8)
            rhs = rhs_v[pl.ds(r, b), c0:c1]
            diag = 4.0 + d_v[pl.ds(r, b), c0:c1]
            near = pl.reciprocal(diag, approx=True)
            dinv = near * (2.0 - diag * near)
            d_v[pl.ds(r, b), c0:c1] = dinv
            fp[pl.ds(r + 8, b), c0 + LANES : c0 + LANES + w] = W1 * dinv * rhs

    def do_second(r0, r1, c0, c1, b):
        w = c1 - c0

        @pl.loop(0, (r1 - r0) // b)
        def _(t):
            r = pl.multiple_of(r0 + t * b, 8)
            beside = halo_sum(fp, r, c0, b, w)
            rhs = rhs_v[pl.ds(r, b), c0:c1]
            dinv = d_v[pl.ds(r, b), c0:c1]
            sp[pl.ds(r + 8, b), c0 + LANES : c0 + LANES + w] = dinv * (CC * rhs + W2 * beside)

    lane = lax.broadcasted_iota(jnp.int32, (8, LANES), 1)
    up_dev = (lax.rem(sx + nsx - 1, nsx), sy)
    down_dev = (lax.rem(sx + 1, nsx), sy)
    left_dev = (sx, lax.rem(sy + nsy - 1, nsy))
    right_dev = (sx, lax.rem(sy + 1, nsy))

    def halo_copies(ph):
        out = []
        for k, dev in enumerate((up_dev, down_dev)):
            out.append(pltpu.make_async_remote_copy(
                row_s.at[ph, k], row_r.at[ph, k], hs_sem.at[ph, k], hr_sem.at[ph, k],
                device_id=dev, device_id_type=MESH))
        for k, dev in enumerate((left_dev, right_dev)):
            out.append(pltpu.make_async_remote_copy(
                col_s.at[ph, k], col_r.at[ph, k], hs_sem.at[ph, 2 + k], hr_sem.at[ph, 2 + k],
                device_id=dev, device_id_type=MESH))
        return out

    def halo_send(ph, ref):
        row_s[ph, 0] = ref[8:9, LANES : LANES + cols]
        row_s[ph, 1] = ref[rows + 7 : rows + 8, LANES : LANES + cols]
        one = jnp.zeros((8, LANES), F32)
        two = jnp.zeros((8, LANES), F32)
        for i in range(rows // 8):
            a = ref[8 + 8 * i : 16 + 8 * i, LANES : 2 * LANES]
            b = ref[8 + 8 * i : 16 + 8 * i, cols : cols + LANES]
            one = jnp.where(lane == i, a[:, 0:1], one)
            two = jnp.where(lane == i, b[:, LANES - 1 : LANES], two)
        col_s[ph, 0] = one
        col_s[ph, 1] = two
        cps = halo_copies(ph)
        for cp in cps:
            cp.start()
        return cps

    def halo_take(ph, ref, cps):
        for cp in cps:
            cp.wait_recv()
        zero_row = jnp.zeros((1, cols), F32)
        ref[7:8, LANES : LANES + cols] = jnp.where(sx > 0, row_r[ph, 1], zero_row)
        ref[rows + 8 : rows + 9, LANES : LANES + cols] = jnp.where(sx < nsx - 1, row_r[ph, 0], zero_row)
        zero = jnp.zeros((8, LANES), F32)
        from_left = jnp.where(sy > 0, col_r[ph, 1], zero)
        from_right = jnp.where(sy < nsy - 1, col_r[ph, 0], zero)
        for i in range(rows // 8):
            ref[8 + 8 * i : 16 + 8 * i, 0:LANES] = jnp.broadcast_to(from_left[:, i : i + 1], (8, LANES))
            ref[8 + 8 * i : 16 + 8 * i, cols + LANES : cols + 2 * LANES] = jnp.broadcast_to(
                from_right[:, i : i + 1], (8, LANES))

    for i in range(4):
        for cp in loads[i]:
            cp.wait()
        do_first(*regions[i], 32 if i < 2 else 16)
    for cp in small:
        cp.wait()
    pl.semaphore_wait(barrier, n - 1)
    for h in range(2):
        for i in range(1, nz):
            send(h, z, y, x, c, (zs[i], y, x, c), ss_z.at[h, i])
    cps0 = halo_send(0, fp)
    ag_first(0)
    for cp in loads[4]:
        cp.wait()
    do_first(*regions[4], 16)
    for i in range(1, nz):
        ag_first(i)
    halo_take(0, fp, cps0)
    do_second(0, rows, *left, 32)
    do_second(0, rows, *right, 32)
    do_second(0, 8, LANES, cols - LANES, 8)
    do_second(rows - 8, rows, LANES, cols - LANES, 8)
    cps1 = halo_send(1, sp)
    for i in range(nz):
        ag_second(i)
    for i in range(5, 4 + chunks):
        for cp in loads[i]:
            cp.wait()
        do_first(*regions[i], 16)
    for i in range(nz):
        ag_third(i)

    index = idx_v[...]
    owner = own_v[...]
    trow = lax.div(index, runs)
    tcol = index - trow * runs
    rid = jnp.where(tcol == 0, trow, jnp.where(tcol == runs - 1, rows + trow, jnp.where(
        trow == 0, 2 * rows + tcol, 2 * rows + runs + tcol)))
    ra = lax.shift_right_logical(rid, 7)
    rbm = rid & (LANES - 1)
    pr = lax.shift_right_logical(owner, 1)
    par = owner & 1
    nblk = tiles // LANES
    stack = jnp.concatenate([v.astype(F32) for v in (ra, rbm, pr, par)]
                            + [jnp.zeros((LANES - 4 * nblk, LANES), F32)], axis=0)
    numbers = stack.T

    halo_take(1, sp, cps1)

    def rim(row, col, nrows, width):
        return ((1.0 - CC) * rhs_v[pl.ds(row, nrows), col : col + width]
                - W2 * halo_sum(fp, row, col, nrows, width) + halo_sum(sp, row, col, nrows, width))

    def put(at, nrows, value):
        cr[pl.ds(at, nrows), :] = value

    @pl.loop(0, rows // 32)
    def _(t):
        r = pl.multiple_of(t * 32, 32)
        one = rim(r, 0, 32, LANES)
        two = rim(r, cols - LANES, 32, LANES)
        put(r, 32, one)
        put(r + rows, 32, two)

    cr[2 * rows :, :] = jnp.zeros((cr.shape[0] - 2 * rows, LANES), F32)
    top = rim(0, 0, 1, cols)
    bottom = rim(rows - 1, 0, 1, cols)
    for k in range(runs):
        put(2 * rows + k, 1, top[:, LANES * k : LANES * k + LANES])
        put(2 * rows + runs + k, 1, bottom[:, LANES * k : LANES * k + LANES])

    nk = cr.shape[0] // LANES

    @pl.loop(0, nk)
    def _(t):
        at = pl.multiple_of(t * LANES, LANES)
        v = cr[pl.ds(at, LANES), :]
        hi = v.astype(BF16)
        rb[pl.ds(at, LANES), 0:LANES] = hi
        rb[pl.ds(at, LANES), LANES:] = (v - hi.astype(F32)).astype(BF16)

    m = 4
    lanes_m = lax.broadcasted_iota(jnp.int32, (m * LANES, LANES), 1).astype(F32)
    zero_b = jnp.zeros((m * LANES, LANES), BF16)
    count = jnp.zeros((LANES, LANES), F32)
    rr = jnp.zeros((8, LANES), F32)
    pq = jnp.zeros((8, LANES), F32)
    qq = jnp.zeros((8, LANES), F32)

    def spread(kind, g):
        return jnp.concatenate([
            jnp.broadcast_to(numbers[:, kind * nblk + g * m + u : kind * nblk + g * m + u + 1],
                             (LANES, LANES)) for u in range(m)], axis=0)

    def fold(v):
        return jnp.sum(v.reshape(-1, 8, LANES), axis=0)

    npair = blocks.shape[1]
    gp = min(npair, 16)
    for g in range(nblk // m):
        at = g * m * LANES
        a32 = spread(0, g)
        a16 = a32.astype(BF16)
        base = jnp.where(spread(1, g) == lanes_m, 1.0, 0.0).astype(BF16)
        aone = jnp.where(a32 == lanes_m, 1.0, 0.0).astype(BF16)
        count += lax.dot_general(base, aone, (((0,), (0,)), ((), ())), preferred_element_type=F32)
        hot = jnp.concatenate([jnp.where(a16 == k, base, zero_b) for k in range(nk)], axis=1)
        both = jnp.dot(hot, rb[...], preferred_element_type=F32)
        r = both[:, :LANES] + both[:, LANES:]
        p_v[at : at + m * LANES, :] = both[:, :LANES].astype(BF16)
        r_out[at : at + m * LANES, :] = r
        rr += fold(r * r)

    ag_last()
    for g in range(nblk // m):
        at = g * m * LANES
        p = p_v[at : at + m * LANES, :]
        r = r_out[at : at + m * LANES, :]
        p16 = spread(2, g).astype(BF16)

        def pairs(k0, acc):
            masked = jnp.concatenate(
                [jnp.where(p16 == (k0 + k if isinstance(k0, int) else (k0 + k).astype(BF16)), p, zero_b)
                 for k in range(gp)], axis=1)
            mats = jnp.concatenate([blocks[0, pl.ds(k0, gp)].reshape(gp * LANES, LANES),
                                    blocks[1, pl.ds(k0, gp)].reshape(gp * LANES, LANES)], axis=1)
            return acc + jnp.dot(masked, mats, preferred_element_type=F32)

        acc = jnp.zeros((m * LANES, 2 * LANES), F32)
        if npair == gp:
            acc = pairs(0, acc)
        else:
            acc = lax.fori_loop(0, npair // gp, lambda s, v: pairs(s * gp, v), acc)
        qb = jnp.where(spread(3, g) > 0.5, acc[:, LANES:], acc[:, :LANES]).astype(BF16)
        q_out[at : at + m * LANES, :] = qb
        q = qb.astype(F32)
        pq += fold(r * q)
        qq += fold(q * q)

    part = jnp.concatenate([jnp.sum(v, axis=0, keepdims=True) for v in (rr, pq, qq)]
                           + [jnp.zeros((5, LANES), F32)], axis=0)
    sum_buf[me] = part

    def sum_copy(slot, k):
        o = lax.rem(me + k, n)
        return pltpu.make_async_remote_copy(
            sum_buf.at[slot], sum_buf.at[slot], sum_s.at[k], sum_r.at[slot],
            device_id=(lax.div(o, nsy), lax.rem(o, nsy)), device_id_type=MESH)

    @pl.loop(1, n)
    def _(k):
        sum_copy(me, k).start()

    do_second(8, rows - 8, LANES, cols - LANES, 16)
    for a in range(nk):
        at = a * LANES
        cr[at : at + LANES, :] = cr[at : at + LANES, :] * count[:, a : a + 1]

    for cp in cps0 + cps1:
        cp.wait_send()
    for cp in sends:
        cp.wait_send()

    @pl.loop(1, n)
    def _(k):
        sum_copy(me, k).wait_send()
        sum_copy(lax.rem(me + k, n), k).wait_recv()

    sums_out[...] = jnp.sum(sum_buf[...], axis=0)


def back_kernel(sp, cr, r_ref, q_ref, sums, out, res, direc,
                left, right, top, bottom, res_v, dir_v, sem):
    rows, cols = out.shape
    tiles = r_ref.shape[0]
    runs = cols // LANES
    inner = pltpu.make_async_copy(
        sp.at[16 : rows, 2 * LANES : cols],
        out.at[8 : rows - 8, LANES : cols - LANES], sem.at[0])
    inner.start()
    copies = [inner]
    total = jnp.sum(sums[...], axis=1, keepdims=True)
    rr, pq, qq = total[0:1], total[1:2], total[2:3]
    alpha = rr / pq
    beta = (rr - 2.0 * alpha * pq + alpha * alpha * qq) / rr

    nch = 4
    size = tiles // nch
    for k in range(nch):
        sl = slice(k * size, (k + 1) * size)

        @pl.loop(0, size // 64)
        def _(t, k=k):
            at = pl.multiple_of(k * size + t * 64, 64)
            r = r_ref[pl.ds(at, 64), :]
            v = r - alpha * q_ref[pl.ds(at, 64), :].astype(F32)
            res_v[pl.ds(at, 64), :] = v
            dir_v[pl.ds(at, 64), :] = v + beta * r

        for src, dst, i in ((res_v, res, 1 + k), (dir_v, direc, 1 + nch + k)):
            cp = pltpu.make_async_copy(src.at[sl], dst.at[sl], sem.at[i])
            cp.start()
            copies.append(cp)

    @pl.loop(0, rows // 64)
    def _(t):
        at = pl.multiple_of(t * 64, 64)
        left[pl.ds(at, 64), :] = sp[pl.ds(at + 8, 64), LANES : 2 * LANES] + alpha * cr[pl.ds(at, 64), :]
        right[pl.ds(at, 64), :] = (sp[pl.ds(at + 8, 64), cols : cols + LANES]
                                   + alpha * cr[pl.ds(at + rows, 64), :])

    top[...] = sp[8:16, 2 * LANES : cols]
    bottom[...] = sp[rows : rows + 8, 2 * LANES : cols]
    for k in range(1, runs - 1):
        sl = slice((k - 1) * LANES, k * LANES)
        top[0:1, sl] = top[0:1, sl] + alpha * cr[2 * rows + k : 2 * rows + k + 1, :]
        bottom[7:8, sl] = bottom[7:8, sl] + alpha * cr[2 * rows + runs + k : 2 * rows + runs + k + 1, :]
    i = 1 + 2 * nch
    for src, dst in ((left, out.at[:, 0:LANES]), (right, out.at[:, cols - LANES : cols]),
                     (top, out.at[0:8, LANES : cols - LANES]),
                     (bottom, out.at[rows - 8 : rows, LANES : cols - LANES])):
        cp = pltpu.make_async_copy(src, dst, sem.at[i])
        cp.start()
        copies.append(cp)
        i += 1
    for cp in copies:
        cp.wait()


def per_device(nsx, nsy, rhs, sigma, tile_list, tile_owner, schur_blocks):
    rows, cols = rhs.shape
    tiles = tile_list.shape[0]
    n = nsx * nsy
    nz, nx = nsx // 2, nsy // 2
    nk = -(-(2 * rows + 2 * (cols // LANES)) // LANES)
    vm = pl.BlockSpec(memory_space=pltpu.VMEM)
    hbm = pl.BlockSpec(memory_space=pl.ANY)
    big = pl.BlockSpec(memory_space=pltpu.HBM)
    dma = pltpu.SemaphoreType.DMA
    padded = (rows + 16, cols + 2 * LANES)
    kept = pltpu.VMEM
    sp, cr, r, q, sums = pl.pallas_call(
        functools.partial(front_kernel, nsx, nsy),
        out_shape=[kept(padded, F32), kept((nk * LANES, LANES), F32), kept((tiles, LANES), F32),
                   kept((tiles, LANES), BF16), kept((8, LANES), F32)],
        in_specs=[big] * 5,
        out_specs=[vm] * 5,
        scratch_shapes=[
            pltpu.VMEM((rows, cols), F32), pltpu.VMEM((rows, cols), F32), pltpu.VMEM(padded, F32),
            pltpu.VMEM((nk * LANES, 2 * LANES), BF16), pltpu.VMEM((2, n // 2, LANES, LANES), BF16),
            pltpu.VMEM((tiles // LANES, LANES), jnp.int32), pltpu.VMEM((tiles // LANES, LANES), jnp.int32),
            pltpu.VMEM((tiles, LANES), BF16),
            pltpu.VMEM((2, 2, 1, cols), F32), pltpu.VMEM((2, 2, 1, cols), F32),
            pltpu.VMEM((2, 2, 8, LANES), F32), pltpu.VMEM((2, 2, 8, LANES), F32),
            pltpu.VMEM((n, 8, LANES), F32),
            dma((2, 8)), dma((3,)), dma((2, 4)), dma((2, 4)), dma((2, n)), dma((2, nz)), dma((2, nz, nx)),
            dma((2, nz, 2, nx)), dma((2, nz, 2, nx)), dma((n,)), dma((n,)),
        ],
        compiler_params=pltpu.CompilerParams(
            collective_id=0, has_side_effects=True, vmem_limit_bytes=44 * 2**20),
        name="front",
    )(*[pltpu.with_memory_space_constraint(v, pltpu.HBM) for v in (
        rhs, sigma, tile_list.reshape(-1, LANES), tile_owner.reshape(-1, LANES),
        schur_blocks.reshape(LANES, LANES))])
    nch = 4
    return pl.pallas_call(
        back_kernel,
        out_shape=[jax.ShapeDtypeStruct((rows, cols), F32), jax.ShapeDtypeStruct((tiles, LANES), F32),
                   jax.ShapeDtypeStruct((tiles, LANES), F32)],
        in_specs=[vm] * 5,
        out_specs=[hbm] * 3,
        scratch_shapes=[
            pltpu.VMEM((rows, LANES), F32), pltpu.VMEM((rows, LANES), F32),
            pltpu.VMEM((8, cols - 2 * LANES), F32), pltpu.VMEM((8, cols - 2 * LANES), F32),
            pltpu.VMEM((tiles, LANES), F32), pltpu.VMEM((tiles, LANES), F32),
            dma((1 + 2 * nch + 4,)),
        ],
        compiler_params=pltpu.CompilerParams(vmem_limit_bytes=16 * 2**20),
        name="back",
    )(sp, cr, r, q, sums)


def solution(mesh):
    nsx, nsy = mesh.shape["sx"], mesh.shape["sy"]
    in_specs = (
        P("sx", "sy"),
        P("sx", "sy"),
        P(("sx", "sy")),
        P(("sx", "sy"), None),
        P(("sx", "sy"), None, None),
    )
    out_specs = (P("sx", "sy"), P(("sx", "sy"), None), P(("sx", "sy"), None))

    def body(*args):
        return tuple(per_device(nsx, nsy, *args))

    return jax.shard_map(body, mesh=mesh, in_specs=in_specs, out_specs=out_specs, check_vma=False)
```

```python
import functools

import jax
import jax.numpy as jnp
from jax import lax
from jax.experimental import pallas as pl
from jax.experimental.pallas import tpu as pltpu
from jax.sharding import PartitionSpec as P

MESH = pl.DeviceIdType.MESH
W1 = 0.6111111
W2 = 2.75
CC = W1 + W2 * (1.0 - W1)
LANES = 128
F32 = jnp.float32
BF16 = jnp.bfloat16


def halo_sum(ref, row, col, rows, width):
    if not isinstance(row, int):
        ref = ref.at[pl.ds(row, rows + 16)]
        row = 0
    wide = ref[row + 8 : row + 8 + rows, col : col + width + 2 * LANES]
    total = width + 2 * LANES
    left = pltpu.roll(wide, 1, 1)[:, LANES : LANES + width]
    right = pltpu.roll(wide, total - 1, 1)[:, LANES : LANES + width]
    up = ref[row + 7 : row + 7 + rows, col + LANES : col + LANES + width]
    down = ref[row + 9 : row + 9 + rows, col + LANES : col + LANES + width]
    return (left + right) + (up + down)


def front_kernel(nsx, nsy, rhs_h, sig_h, sch_ref, sp, cr, blocks,
                 rhs_v, d_v, fp, row_s, row_r, col_s, col_r,
                 in_sem, small_sem, hs_sem, hr_sem, ag_r, ss_z, ss_y, ss_x, ss_c):
    rows, cols = rhs_v.shape
    runs = cols // LANES
    nz, nx = nsx // 2, nsy // 2
    n = nsx * nsy
    sx = lax.axis_index("sx")
    sy = lax.axis_index("sy")
    me = sx * nsy + sy
    z, y = lax.div(sx, 2), lax.rem(sx, 2)
    x, c = lax.div(sy, 2), lax.rem(sy, 2)

    left, right = (0, 2 * LANES), (cols - 2 * LANES, cols)
    regions = [(0, rows) + left, (0, rows) + right,
               (0, 16, left[1], right[0]), (rows - 16, rows, left[1], right[0])]
    chunks = 4
    step = (rows - 32) // chunks // 16 * 16
    cuts = [16 + step * i for i in range(chunks)] + [rows - 16]
    for i in range(chunks):
        regions.append((cuts[i], cuts[i + 1], left[1], right[0]))
    loads = []
    for i, (r0, r1, c0, c1) in enumerate(regions):
        pair = []
        for k, (src, dst) in enumerate(((rhs_h, rhs_v), (sig_h, d_v))):
            cp = pltpu.make_async_copy(src.at[r0:r1, c0:c1], dst.at[r0:r1, c0:c1], in_sem.at[k, i])
            cp.start()
            pair.append(cp)
        loads.append(pair)

    barrier = pltpu.get_barrier_semaphore()

    @pl.loop(1, n)
    def _(k):
        o = lax.rem(me + k, n)
        pl.semaphore_signal(barrier, inc=1, device_id=(lax.div(o, nsy), lax.rem(o, nsy)),
                            device_id_type=MESH)

    own = pltpu.make_async_copy(sch_ref, blocks.at[c, (2 * z + y) * nx + x], small_sem)
    own.start()

    half = LANES // 2

    def piece(h, zz, yy, xx, cc, dev, sem):
        pair = (2 * zz + yy) * nx + xx
        ref = blocks.at[cc, pair, pl.ds(h * half, half), :]
        dz, dy, dx, dc = dev
        return pltpu.make_async_remote_copy(
            ref, ref, sem, ag_r.at[h, 2 * pair + cc],
            device_id=(2 * dz + dy, 2 * dx + dc), device_id_type=MESH)

    sends = []

    def send(*args):
        cp = piece(*args)
        cp.start()
        sends.append(cp)

    def arrived(h, zz, yy, xx, cc):
        piece(h, zz, yy, xx, cc, (z, y, x, 1 - c), ss_c.at[0, 0, 0, 0]).wait_recv()

    zs = [lax.rem(z + k, nz) for k in range(nz)]
    ys = [y, 1 - y]
    xs = [lax.rem(x + k, nx) for k in range(nx)]

    def to_core(h, i, j, k):
        send(h, zs[i], ys[j], xs[k], c, (z, y, x, 1 - c), ss_c.at[h, i, j, k])

    def ag_first(i):
        for h in range(2):
            if i:
                arrived(h, zs[i], y, x, c)
            if h == 0:
                send(0, zs[i], y, x, c, (z, 1 - y, x, c), ss_y.at[0, i, 0])
            for k in range(1, nx):
                send(h, zs[i], y, x, c, (z, y, xs[k], c), ss_x.at[h, i, 0, k])
            if h == 1:
                send(1, zs[i], y, x, c, (z, 1 - y, x, c), ss_y.at[1, i, 0])
            to_core(h, i, 0, 0)

    def ag_second(i):
        arrived(0, zs[i], 1 - y, x, c)
        for k in range(1, nx):
            send(0, zs[i], 1 - y, x, c, (z, y, xs[k], c), ss_x.at[0, i, 1, k])
        to_core(0, i, 1, 0)
        for k in range(1, nx):
            arrived(1, zs[i], y, xs[k], c)
            send(1, zs[i], y, xs[k], c, (z, 1 - y, x, c), ss_y.at[1, i, k])
            to_core(1, i, 0, k)

    def ag_third(i):
        for k in range(1, nx):
            arrived(0, zs[i], y, xs[k], c)
            to_core(0, i, 0, k)
            arrived(0, zs[i], 1 - y, xs[k], c)
            to_core(0, i, 1, k)
        for k in range(nx):
            arrived(1, zs[i], 1 - y, xs[k], c)
            to_core(1, i, 1, k)

    def ag_last():
        for h in range(2):
            for i in range(nz):
                for j in range(2):
                    for k in range(nx):
                        arrived(h, zs[i], ys[j], xs[k], 1 - c)

    def do_first(r0, r1, c0, c1, b):
        w = c1 - c0

        @pl.loop(0, (r1 - r0) // b)
        def _(t):
            r = pl.multiple_of(r0 + t * b, 8)
            rhs = rhs_v[pl.ds(r, b), c0:c1]
            diag = 4.0 + d_v[pl.ds(r, b), c0:c1]
            near = pl.reciprocal(diag, approx=True)
            dinv = near * (2.0 - diag * near)
            d_v[pl.ds(r, b), c0:c1] = dinv
            fp[pl.ds(r + 8, b), c0 + LANES : c0 + LANES + w] = W1 * dinv * rhs

    def do_second(r0, r1, c0, c1, b):
        w = c1 - c0

        @pl.loop(0, (r1 - r0) // b)
        def _(t):
            r = pl.multiple_of(r0 + t * b, 8)
            beside = halo_sum(fp, r, c0, b, w)
            rhs = rhs_v[pl.ds(r, b), c0:c1]
            dinv = d_v[pl.ds(r, b), c0:c1]
            sp[pl.ds(r + 8, b), c0 + LANES : c0 + LANES + w] = dinv * (CC * rhs + W2 * beside)

    lane = lax.broadcasted_iota(jnp.int32, (8, LANES), 1)
    up_dev = (lax.rem(sx + nsx - 1, nsx), sy)
    down_dev = (lax.rem(sx + 1, nsx), sy)
    left_dev = (sx, lax.rem(sy + nsy - 1, nsy))
    right_dev = (sx, lax.rem(sy + 1, nsy))

    def halo_copies(ph):
        out = []
        for k, dev in enumerate((up_dev, down_dev)):
            out.append(pltpu.make_async_remote_copy(
                row_s.at[ph, k], row_r.at[ph, k], hs_sem.at[ph, k], hr_sem.at[ph, k],
                device_id=dev, device_id_type=MESH))
        for k, dev in enumerate((left_dev, right_dev)):
            out.append(pltpu.make_async_remote_copy(
                col_s.at[ph, k], col_r.at[ph, k], hs_sem.at[ph, 2 + k], hr_sem.at[ph, 2 + k],
                device_id=dev, device_id_type=MESH))
        return out

    def halo_send(ph, ref):
        row_s[ph, 0] = ref[8:9, LANES : LANES + cols]
        row_s[ph, 1] = ref[rows + 7 : rows + 8, LANES : LANES + cols]
        one = jnp.zeros((8, LANES), F32)
        two = jnp.zeros((8, LANES), F32)
        for i in range(rows // 8):
            a = ref[8 + 8 * i : 16 + 8 * i, LANES : 2 * LANES]
            b = ref[8 + 8 * i : 16 + 8 * i, cols : cols + LANES]
            one = jnp.where(lane == i, a[:, 0:1], one)
            two = jnp.where(lane == i, b[:, LANES - 1 : LANES], two)
        col_s[ph, 0] = one
        col_s[ph, 1] = two
        cps = halo_copies(ph)
        for cp in cps:
            cp.start()
        return cps

    def halo_take(ph, ref, cps):
        for cp in cps:
            cp.wait_recv()
        zero_row = jnp.zeros((1, cols), F32)
        ref[7:8, LANES : LANES + cols] = jnp.where(sx > 0, row_r[ph, 1], zero_row)
        ref[rows + 8 : rows + 9, LANES : LANES + cols] = jnp.where(sx < nsx - 1, row_r[ph, 0], zero_row)
        zero = jnp.zeros((8, LANES), F32)
        from_left = jnp.where(sy > 0, col_r[ph, 1], zero)
        from_right = jnp.where(sy < nsy - 1, col_r[ph, 0], zero)
        for i in range(rows // 8):
            ref[8 + 8 * i : 16 + 8 * i, 0:LANES] = jnp.broadcast_to(from_left[:, i : i + 1], (8, LANES))
            ref[8 + 8 * i : 16 + 8 * i, cols + LANES : cols + 2 * LANES] = jnp.broadcast_to(
                from_right[:, i : i + 1], (8, LANES))

    for i in range(4):
        for cp in loads[i]:
            cp.wait()
        do_first(*regions[i], 32 if i < 2 else 16)
    own.wait()
    pl.semaphore_wait(barrier, n - 1)
    for h in range(2):
        for i in range(1, nz):
            send(h, z, y, x, c, (zs[i], y, x, c), ss_z.at[h, i])
    cps0 = halo_send(0, fp)
    ag_first(0)
    for cp in loads[4]:
        cp.wait()
    do_first(*regions[4], 16)
    for i in range(1, nz):
        ag_first(i)
    halo_take(0, fp, cps0)
    do_second(0, rows, *left, 32)
    do_second(0, rows, *right, 32)
    do_second(0, 8, LANES, cols - LANES, 8)
    do_second(rows - 8, rows, LANES, cols - LANES, 8)
    cps1 = halo_send(1, sp)
    for i in range(nz):
        ag_second(i)
    for i in range(5, 4 + chunks):
        for cp in loads[i]:
            cp.wait()
        do_first(*regions[i], 16)
    for i in range(nz):
        ag_third(i)

    halo_take(1, sp, cps1)

    def rim(row, col, nrows, width):
        return ((1.0 - CC) * rhs_v[pl.ds(row, nrows), col : col + width]
                - W2 * halo_sum(fp, row, col, nrows, width) + halo_sum(sp, row, col, nrows, width))

    def put(at, nrows, value):
        cr[pl.ds(at, nrows), :] = value

    @pl.loop(0, rows // 32)
    def _(t):
        r = pl.multiple_of(t * 32, 32)
        one = rim(r, 0, 32, LANES)
        two = rim(r, cols - LANES, 32, LANES)
        put(r, 32, one)
        put(r + rows, 32, two)

    cr[2 * rows :, :] = jnp.zeros((cr.shape[0] - 2 * rows, LANES), F32)
    top = rim(0, 0, 1, cols)
    bottom = rim(rows - 1, 0, 1, cols)
    for k in range(runs):
        put(2 * rows + k, 1, top[:, LANES * k : LANES * k + LANES])
        put(2 * rows + runs + k, 1, bottom[:, LANES * k : LANES * k + LANES])

    do_second(8, rows - 8, LANES, cols - LANES, 16)
    ag_last()
    for cp in cps0 + cps1:
        cp.wait_send()
    for cp in sends:
        cp.wait_send()


def product_kernel(rows, runs, idx_ref, own_ref, rim_ref, blocks, r_out, q_out, part_out, count_out, rb, p_v, idx_v, own_v, sem):
    tiles = r_out.shape[0]
    pair = [pltpu.make_async_copy(a, b, sem.at[i])
            for i, (a, b) in enumerate(((idx_ref, idx_v), (own_ref, own_v)))]
    for cp in pair:
        cp.start()
    for cp in pair:
        cp.wait()

    index = idx_v[...]
    owner = own_v[...]
    trow = lax.div(index, runs)
    tcol = index - trow * runs
    rid = jnp.where(tcol == 0, trow, jnp.where(tcol == runs - 1, rows + trow, jnp.where(
        trow == 0, 2 * rows + tcol, 2 * rows + runs + tcol)))
    ra = lax.shift_right_logical(rid, 7)
    rbm = rid & (LANES - 1)
    pr = lax.shift_right_logical(owner, 1)
    par = owner & 1
    nblk = tiles // LANES
    stack = jnp.concatenate([v.astype(F32) for v in (ra, rbm, pr, par)]
                            + [jnp.zeros((LANES - 4 * nblk, LANES), F32)], axis=0)
    numbers = stack.T

    nk = rim_ref.shape[0] // LANES

    @pl.loop(0, nk)
    def _(t):
        at = pl.multiple_of(t * LANES, LANES)
        v = rim_ref[pl.ds(at, LANES), :]
        hi = v.astype(BF16)
        rb[pl.ds(at, LANES), 0:LANES] = hi
        rb[pl.ds(at, LANES), LANES:] = (v - hi.astype(F32)).astype(BF16)

    m = 4
    lanes_m = lax.broadcasted_iota(jnp.int32, (m * LANES, LANES), 1).astype(F32)
    zero_b = jnp.zeros((m * LANES, LANES), BF16)
    count = jnp.zeros((LANES, LANES), F32)
    rr = jnp.zeros((8, LANES), F32)
    pq = jnp.zeros((8, LANES), F32)
    qq = jnp.zeros((8, LANES), F32)

    def spread(kind, g):
        return jnp.concatenate([
            jnp.broadcast_to(numbers[:, kind * nblk + g * m + u : kind * nblk + g * m + u + 1],
                             (LANES, LANES)) for u in range(m)], axis=0)

    def fold(v):
        return jnp.sum(v.reshape(-1, 8, LANES), axis=0)

    npair = blocks.shape[1]
    gp = min(npair, 16)
    for g in range(nblk // m):
        at = g * m * LANES
        a32 = spread(0, g)
        a16 = a32.astype(BF16)
        base = jnp.where(spread(1, g) == lanes_m, 1.0, 0.0).astype(BF16)
        aone = jnp.where(a32 == lanes_m, 1.0, 0.0).astype(BF16)
        count += lax.dot_general(base, aone, (((0,), (0,)), ((), ())), preferred_element_type=F32)
        hot = jnp.concatenate([jnp.where(a16 == k, base, zero_b) for k in range(nk)], axis=1)
        both = jnp.dot(hot, rb[...], preferred_element_type=F32)
        r = both[:, :LANES] + both[:, LANES:]
        p_v[at : at + m * LANES, :] = both[:, :LANES].astype(BF16)
        r_out[at : at + m * LANES, :] = r
        rr += fold(r * r)

    for g in range(nblk // m):
        at = g * m * LANES
        p = p_v[at : at + m * LANES, :]
        r = r_out[at : at + m * LANES, :]
        p16 = spread(2, g).astype(BF16)

        def pairs(k0, acc):
            masked = jnp.concatenate(
                [jnp.where(p16 == k0 + k, p, zero_b)
                 for k in range(gp)], axis=1)
            mats = jnp.concatenate([blocks[0, pl.ds(k0, gp)].reshape(gp * LANES, LANES),
                                    blocks[1, pl.ds(k0, gp)].reshape(gp * LANES, LANES)], axis=1)
            return acc + jnp.dot(masked, mats, preferred_element_type=F32)

        acc = jnp.zeros((m * LANES, 2 * LANES), F32)
        for k0 in range(0, npair, gp):
            acc = pairs(k0, acc)
        qb = jnp.where(spread(3, g) > 0.5, acc[:, LANES:], acc[:, :LANES]).astype(BF16)
        q_out[at : at + m * LANES, :] = qb
        q = qb.astype(F32)
        pq += fold(r * q)
        qq += fold(q * q)

    part_out[...] = jnp.concatenate([jnp.sum(v, axis=0, keepdims=True) for v in (rr, pq, qq)]
                                    + [jnp.zeros((5, LANES), F32)], axis=0)
    count_out[...] = count


def sum_kernel(nsx, nsy, part, rim_ref, count, cr, sums_out, sum_buf, sum_s, sum_r):
    n = nsx * nsy
    me = lax.axis_index("sx") * nsy + lax.axis_index("sy")
    barrier = pltpu.get_barrier_semaphore()

    @pl.loop(1, n)
    def _(k):
        o = lax.rem(me + k, n)
        pl.semaphore_signal(barrier, inc=1, device_id=(lax.div(o, nsy), lax.rem(o, nsy)),
                            device_id_type=MESH)

    sum_buf[me] = part[...]
    pl.semaphore_wait(barrier, n - 1)

    def sum_copy(slot, k):
        o = lax.rem(me + k, n)
        return pltpu.make_async_remote_copy(
            sum_buf.at[slot], sum_buf.at[slot], sum_s.at[k], sum_r.at[slot],
            device_id=(lax.div(o, nsy), lax.rem(o, nsy)), device_id_type=MESH)

    @pl.loop(1, n)
    def _(k):
        sum_copy(me, k).start()

    for a in range(cr.shape[0] // LANES):
        at = a * LANES
        cr[at : at + LANES, :] = rim_ref[at : at + LANES, :] * count[:, a : a + 1]

    @pl.loop(1, n)
    def _(k):
        sum_copy(me, k).wait_send()
        sum_copy(lax.rem(me + k, n), k).wait_recv()

    sums_out[...] = jnp.sum(sum_buf[...], axis=0)


def back_kernel(sp, cr, r_ref, q_ref, sums, out, res, direc,
                left, right, top, bottom, res_v, dir_v, sem):
    rows, cols = out.shape
    tiles = r_ref.shape[0]
    runs = cols // LANES
    inner = pltpu.make_async_copy(
        sp.at[16 : rows, 2 * LANES : cols],
        out.at[8 : rows - 8, LANES : cols - LANES], sem.at[0])
    inner.start()
    copies = [inner]
    total = jnp.sum(sums[...], axis=1, keepdims=True)
    rr, pq, qq = total[0:1], total[1:2], total[2:3]
    alpha = rr / pq
    beta = (rr - 2.0 * alpha * pq + alpha * alpha * qq) / rr

    nch = 4
    size = tiles // nch
    for k in range(nch):
        sl = slice(k * size, (k + 1) * size)

        @pl.loop(0, size // 64)
        def _(t, k=k):
            at = pl.multiple_of(k * size + t * 64, 64)
            r = r_ref[pl.ds(at, 64), :]
            v = r - alpha * q_ref[pl.ds(at, 64), :].astype(F32)
            res_v[pl.ds(at, 64), :] = v
            dir_v[pl.ds(at, 64), :] = v + beta * r

        for src, dst, i in ((res_v, res, 1 + k), (dir_v, direc, 1 + nch + k)):
            cp = pltpu.make_async_copy(src.at[sl], dst.at[sl], sem.at[i])
            cp.start()
            copies.append(cp)

    @pl.loop(0, rows // 64)
    def _(t):
        at = pl.multiple_of(t * 64, 64)
        left[pl.ds(at, 64), :] = sp[pl.ds(at + 8, 64), LANES : 2 * LANES] + alpha * cr[pl.ds(at, 64), :]
        right[pl.ds(at, 64), :] = (sp[pl.ds(at + 8, 64), cols : cols + LANES]
                                   + alpha * cr[pl.ds(at + rows, 64), :])

    top[...] = sp[8:16, 2 * LANES : cols]
    bottom[...] = sp[rows : rows + 8, 2 * LANES : cols]
    for k in range(1, runs - 1):
        sl = slice((k - 1) * LANES, k * LANES)
        top[0:1, sl] = top[0:1, sl] + alpha * cr[2 * rows + k : 2 * rows + k + 1, :]
        bottom[7:8, sl] = bottom[7:8, sl] + alpha * cr[2 * rows + runs + k : 2 * rows + runs + k + 1, :]
    i = 1 + 2 * nch
    for src, dst in ((left, out.at[:, 0:LANES]), (right, out.at[:, cols - LANES : cols]),
                     (top, out.at[0:8, LANES : cols - LANES]),
                     (bottom, out.at[rows - 8 : rows, LANES : cols - LANES])):
        cp = pltpu.make_async_copy(src, dst, sem.at[i])
        cp.start()
        copies.append(cp)
        i += 1
    for cp in copies:
        cp.wait()


def per_device(nsx, nsy, rhs, sigma, tile_list, tile_owner, schur_blocks):
    rows, cols = rhs.shape
    tiles = tile_list.shape[0]
    n = nsx * nsy
    nz, nx = nsx // 2, nsy // 2
    nk = -(-(2 * rows + 2 * (cols // LANES)) // LANES)
    vm = pl.BlockSpec(memory_space=pltpu.VMEM)
    hbm = pl.BlockSpec(memory_space=pl.ANY)
    big = pl.BlockSpec(memory_space=pltpu.HBM)
    dma = pltpu.SemaphoreType.DMA
    padded = (rows + 16, cols + 2 * LANES)
    kept = pltpu.VMEM

    def in_hbm(v):
        return pltpu.with_memory_space_constraint(v, pltpu.HBM)

    sp, rim, blocks = pl.pallas_call(
        functools.partial(front_kernel, nsx, nsy),
        out_shape=[kept(padded, F32), kept((nk * LANES, LANES), F32), kept((2, n // 2, LANES, LANES), BF16)],
        in_specs=[big] * 3,
        out_specs=[vm] * 3,
        scratch_shapes=[
            pltpu.VMEM((rows, cols), F32), pltpu.VMEM((rows, cols), F32), pltpu.VMEM(padded, F32),
            pltpu.VMEM((2, 2, 1, cols), F32), pltpu.VMEM((2, 2, 1, cols), F32),
            pltpu.VMEM((2, 2, 8, LANES), F32), pltpu.VMEM((2, 2, 8, LANES), F32),
            dma((2, 8)), dma, dma((2, 4)), dma((2, 4)), dma((2, n)), dma((2, nz)), dma((2, nz, nx)),
            dma((2, nz, 2, nx)), dma((2, nz, 2, nx)),
        ],
        compiler_params=pltpu.CompilerParams(
            collective_id=0, has_side_effects=True, vmem_limit_bytes=32 * 2**20),
        name="front",
    )(in_hbm(rhs), in_hbm(sigma), in_hbm(schur_blocks.reshape(LANES, LANES)))
    r, q, part, count = pl.pallas_call(
        functools.partial(product_kernel, rows, cols // LANES),
        out_shape=[kept((tiles, LANES), F32), kept((tiles, LANES), BF16), kept((8, LANES), F32),
                   kept((LANES, LANES), F32)],
        in_specs=[big, big, vm, vm],
        out_specs=[vm] * 4,
        scratch_shapes=[pltpu.VMEM((nk * LANES, 2 * LANES), BF16), pltpu.VMEM((tiles, LANES), BF16),
                        pltpu.VMEM((tiles // LANES, LANES), jnp.int32),
                        pltpu.VMEM((tiles // LANES, LANES), jnp.int32), dma((2,))],
        compiler_params=pltpu.CompilerParams(vmem_limit_bytes=24 * 2**20),
        name="products",
    )(in_hbm(tile_list.reshape(-1, LANES)), in_hbm(tile_owner.reshape(-1, LANES)), rim, blocks)
    cr, sums = pl.pallas_call(
        functools.partial(sum_kernel, nsx, nsy),
        out_shape=[kept((nk * LANES, LANES), F32), kept((8, LANES), F32)],
        in_specs=[vm] * 3,
        out_specs=[vm] * 2,
        scratch_shapes=[pltpu.VMEM((n, 8, LANES), F32), dma((n,)), dma((n,))],
        compiler_params=pltpu.CompilerParams(
            collective_id=1, has_side_effects=True, vmem_limit_bytes=4 * 2**20),
        name="sums",
    )(part, rim, count)
    nch = 4
    return pl.pallas_call(
        back_kernel,
        out_shape=[jax.ShapeDtypeStruct((rows, cols), F32), jax.ShapeDtypeStruct((tiles, LANES), F32),
                   jax.ShapeDtypeStruct((tiles, LANES), F32)],
        in_specs=[vm] * 5,
        out_specs=[hbm] * 3,
        scratch_shapes=[
            pltpu.VMEM((rows, LANES), F32), pltpu.VMEM((rows, LANES), F32),
            pltpu.VMEM((8, cols - 2 * LANES), F32), pltpu.VMEM((8, cols - 2 * LANES), F32),
            pltpu.VMEM((tiles, LANES), F32), pltpu.VMEM((tiles, LANES), F32),
            dma((1 + 2 * nch + 4,)),
        ],
        compiler_params=pltpu.CompilerParams(vmem_limit_bytes=16 * 2**20),
        name="back",
    )(sp, cr, r, q, sums)


def solution(mesh):
    nsx, nsy = mesh.shape["sx"], mesh.shape["sy"]
    in_specs = (
        P("sx", "sy"),
        P("sx", "sy"),
        P(("sx", "sy")),
        P(("sx", "sy"), None),
        P(("sx", "sy"), None, None),
    )
    out_specs = (P("sx", "sy"), P(("sx", "sy"), None), P(("sx", "sy"), None))

    def body(*args):
        return tuple(per_device(nsx, nsy, *args))

    return jax.shard_map(body, mesh=mesh, in_specs=in_specs, out_specs=out_specs, check_vma=False)
```

```python
import functools

import jax
import jax.numpy as jnp
from jax import lax
from jax.experimental import pallas as pl
from jax.experimental.pallas import tpu as pltpu
from jax.sharding import PartitionSpec as P

MESH = pl.DeviceIdType.MESH
W1 = 0.6111111
W2 = 2.75
CC = W1 + W2 * (1.0 - W1)
LANES = 128
F32 = jnp.float32
BF16 = jnp.bfloat16


def halo_sum(ref, row, col, rows, width):
    if not isinstance(row, int):
        ref = ref.at[pl.ds(row, rows + 16)]
        row = 0
    wide = ref[row + 8 : row + 8 + rows, col : col + width + 2 * LANES]
    total = width + 2 * LANES
    left = pltpu.roll(wide, 1, 1)[:, LANES : LANES + width]
    right = pltpu.roll(wide, total - 1, 1)[:, LANES : LANES + width]
    up = ref[row + 7 : row + 7 + rows, col + LANES : col + LANES + width]
    down = ref[row + 9 : row + 9 + rows, col + LANES : col + LANES + width]
    return (left + right) + (up + down)


def front_kernel(nsx, nsy, rhs_h, sig_h, sp, cr,
                 rhs_v, d_v, fp, row_s, row_r, col_s, col_r,
                 in_sem, hs_sem, hr_sem):
    rows, cols = rhs_v.shape
    runs = cols // LANES
    sx = lax.axis_index("sx")
    sy = lax.axis_index("sy")

    left, right = (0, 2 * LANES), (cols - 2 * LANES, cols)
    regions = [(0, rows) + left, (0, rows) + right,
               (0, 16, left[1], right[0]), (rows - 16, rows, left[1], right[0])]
    chunks = 4
    step = (rows - 32) // chunks // 16 * 16
    cuts = [16 + step * i for i in range(chunks)] + [rows - 16]
    for i in range(chunks):
        regions.append((cuts[i], cuts[i + 1], left[1], right[0]))
    loads = []
    for i, (r0, r1, c0, c1) in enumerate(regions):
        pair = []
        for k, (src, dst) in enumerate(((rhs_h, rhs_v), (sig_h, d_v))):
            cp = pltpu.make_async_copy(src.at[r0:r1, c0:c1], dst.at[r0:r1, c0:c1], in_sem.at[k, i])
            cp.start()
            pair.append(cp)
        loads.append(pair)

    def do_first(r0, r1, c0, c1, b):
        w = c1 - c0

        @pl.loop(0, (r1 - r0) // b)
        def _(t):
            r = pl.multiple_of(r0 + t * b, 8)
            rhs = rhs_v[pl.ds(r, b), c0:c1]
            diag = 4.0 + d_v[pl.ds(r, b), c0:c1]
            near = pl.reciprocal(diag, approx=True)
            dinv = near * (2.0 - diag * near)
            d_v[pl.ds(r, b), c0:c1] = dinv
            fp[pl.ds(r + 8, b), c0 + LANES : c0 + LANES + w] = W1 * dinv * rhs

    def do_second(r0, r1, c0, c1, b):
        w = c1 - c0

        @pl.loop(0, (r1 - r0) // b)
        def _(t):
            r = pl.multiple_of(r0 + t * b, 8)
            beside = halo_sum(fp, r, c0, b, w)
            rhs = rhs_v[pl.ds(r, b), c0:c1]
            dinv = d_v[pl.ds(r, b), c0:c1]
            sp[pl.ds(r + 8, b), c0 + LANES : c0 + LANES + w] = dinv * (CC * rhs + W2 * beside)

    lane = lax.broadcasted_iota(jnp.int32, (8, LANES), 1)
    up_dev = (lax.rem(sx + nsx - 1, nsx), sy)
    down_dev = (lax.rem(sx + 1, nsx), sy)
    left_dev = (sx, lax.rem(sy + nsy - 1, nsy))
    right_dev = (sx, lax.rem(sy + 1, nsy))

    barrier = pltpu.get_barrier_semaphore()
    for dev in (up_dev, down_dev, left_dev, right_dev):
        pl.semaphore_signal(barrier, inc=1, device_id=dev, device_id_type=MESH)

    def halo_copies(ph):
        out = []
        for k, dev in enumerate((up_dev, down_dev)):
            out.append(pltpu.make_async_remote_copy(
                row_s.at[ph, k], row_r.at[ph, k], hs_sem.at[ph, k], hr_sem.at[ph, k],
                device_id=dev, device_id_type=MESH))
        for k, dev in enumerate((left_dev, right_dev)):
            out.append(pltpu.make_async_remote_copy(
                col_s.at[ph, k], col_r.at[ph, k], hs_sem.at[ph, 2 + k], hr_sem.at[ph, 2 + k],
                device_id=dev, device_id_type=MESH))
        return out

    def halo_send(ph, ref):
        row_s[ph, 0] = ref[8:9, LANES : LANES + cols]
        row_s[ph, 1] = ref[rows + 7 : rows + 8, LANES : LANES + cols]
        one = jnp.zeros((8, LANES), F32)
        two = jnp.zeros((8, LANES), F32)
        for i in range(rows // 8):
            a = ref[8 + 8 * i : 16 + 8 * i, LANES : 2 * LANES]
            b = ref[8 + 8 * i : 16 + 8 * i, cols : cols + LANES]
            one = jnp.where(lane == i, a[:, 0:1], one)
            two = jnp.where(lane == i, b[:, LANES - 1 : LANES], two)
        col_s[ph, 0] = one
        col_s[ph, 1] = two
        cps = halo_copies(ph)
        for cp in cps:
            cp.start()
        return cps

    def halo_take(ph, ref, cps):
        for cp in cps:
            cp.wait_recv()
        zero_row = jnp.zeros((1, cols), F32)
        ref[7:8, LANES : LANES + cols] = jnp.where(sx > 0, row_r[ph, 1], zero_row)
        ref[rows + 8 : rows + 9, LANES : LANES + cols] = jnp.where(sx < nsx - 1, row_r[ph, 0], zero_row)
        zero = jnp.zeros((8, LANES), F32)
        from_left = jnp.where(sy > 0, col_r[ph, 1], zero)
        from_right = jnp.where(sy < nsy - 1, col_r[ph, 0], zero)
        for i in range(rows // 8):
            ref[8 + 8 * i : 16 + 8 * i, 0:LANES] = jnp.broadcast_to(from_left[:, i : i + 1], (8, LANES))
            ref[8 + 8 * i : 16 + 8 * i, cols + LANES : cols + 2 * LANES] = jnp.broadcast_to(
                from_right[:, i : i + 1], (8, LANES))

    for i in range(4):
        for cp in loads[i]:
            cp.wait()
        do_first(*regions[i], 32 if i < 2 else 16)
    pl.semaphore_wait(barrier, 4)
    cps0 = halo_send(0, fp)
    for i in range(4, 4 + chunks):
        for cp in loads[i]:
            cp.wait()
        do_first(*regions[i], 16)
    halo_take(0, fp, cps0)
    do_second(0, rows, *left, 32)
    do_second(0, rows, *right, 32)
    do_second(0, 8, LANES, cols - LANES, 8)
    do_second(rows - 8, rows, LANES, cols - LANES, 8)
    cps1 = halo_send(1, sp)
    do_second(8, rows - 8, LANES, cols - LANES, 16)

    halo_take(1, sp, cps1)

    def rim(row, col, nrows, width):
        return ((1.0 - CC) * rhs_v[pl.ds(row, nrows), col : col + width]
                - W2 * halo_sum(fp, row, col, nrows, width) + halo_sum(sp, row, col, nrows, width))

    def put(at, nrows, value):
        cr[pl.ds(at, nrows), :] = value

    @pl.loop(0, rows // 32)
    def _(t):
        r = pl.multiple_of(t * 32, 32)
        one = rim(r, 0, 32, LANES)
        two = rim(r, cols - LANES, 32, LANES)
        put(r, 32, one)
        put(r + rows, 32, two)

    cr[2 * rows :, :] = jnp.zeros((cr.shape[0] - 2 * rows, LANES), F32)
    top = rim(0, 0, 1, cols)
    bottom = rim(rows - 1, 0, 1, cols)
    for k in range(runs):
        put(2 * rows + k, 1, top[:, LANES * k : LANES * k + LANES])
        put(2 * rows + runs + k, 1, bottom[:, LANES * k : LANES * k + LANES])

    for cp in cps0 + cps1:
        cp.wait_send()


def product_kernel(nsx, nsy, rows, runs, idx_ref, own_ref, blocks_h, rim_ref, cr, r_out, q_out, sums_out,
                   rb, p_v, idx_v, own_v, blocks, one_buf, two_buf, sem, one_s, one_r, two_s, two_r):
    sx = lax.axis_index("sx")
    sy = lax.axis_index("sy")
    barrier = pltpu.get_barrier_semaphore()
    for k in range(1, nsy):
        pl.semaphore_signal(barrier, inc=1, device_id=(sx, lax.rem(sy + k, nsy)), device_id_type=MESH)
    for k in range(1, nsx):
        pl.semaphore_signal(barrier, inc=1, device_id=(lax.rem(sx + k, nsx), sy), device_id_type=MESH)
    tiles = r_out.shape[0]
    pair = [pltpu.make_async_copy(a, b, sem.at[i])
            for i, (a, b) in enumerate(((idx_ref, idx_v), (own_ref, own_v)))]
    fetch = pltpu.make_async_copy(blocks_h, blocks, sem.at[2])
    for cp in pair:
        cp.start()
    fetch.start()
    for cp in pair:
        cp.wait()

    index = idx_v[...]
    owner = own_v[...]
    trow = lax.div(index, runs)
    tcol = index - trow * runs
    rid = jnp.where(tcol == 0, trow, jnp.where(tcol == runs - 1, rows + trow, jnp.where(
        trow == 0, 2 * rows + tcol, 2 * rows + runs + tcol)))
    ra = lax.shift_right_logical(rid, 7)
    rbm = rid & (LANES - 1)
    pr = lax.shift_right_logical(owner, 1)
    par = owner & 1
    nblk = tiles // LANES
    stack = jnp.concatenate([v.astype(F32) for v in (ra, rbm, pr, par)]
                            + [jnp.zeros((LANES - 4 * nblk, LANES), F32)], axis=0)
    numbers = stack.T

    nk = rim_ref.shape[0] // LANES

    @pl.loop(0, nk)
    def _(t):
        at = pl.multiple_of(t * LANES, LANES)
        v = rim_ref[pl.ds(at, LANES), :]
        hi = v.astype(BF16)
        rb[pl.ds(at, LANES), 0:LANES] = hi
        rb[pl.ds(at, LANES), LANES:] = (v - hi.astype(F32)).astype(BF16)

    m = 4
    lanes_m = lax.broadcasted_iota(jnp.int32, (m * LANES, LANES), 1).astype(F32)
    zero_b = jnp.zeros((m * LANES, LANES), BF16)
    count = jnp.zeros((LANES, LANES), F32)
    rr = jnp.zeros((8, LANES), F32)
    pq = jnp.zeros((8, LANES), F32)
    qq = jnp.zeros((8, LANES), F32)

    def spread(kind, g):
        return jnp.concatenate([
            jnp.broadcast_to(numbers[:, kind * nblk + g * m + u : kind * nblk + g * m + u + 1],
                             (LANES, LANES)) for u in range(m)], axis=0)

    def fold(v):
        return jnp.sum(v.reshape(-1, 8, LANES), axis=0)

    npair = blocks.shape[0] // 2
    gp = min(npair, 16)
    for g in range(nblk // m):
        at = g * m * LANES
        a32 = spread(0, g)
        a16 = a32.astype(BF16)
        base = jnp.where(spread(1, g) == lanes_m, 1.0, 0.0).astype(BF16)
        aone = jnp.where(a32 == lanes_m, 1.0, 0.0).astype(BF16)
        count += lax.dot_general(base, aone, (((0,), (0,)), ((), ())), preferred_element_type=F32)
        hot = jnp.concatenate([jnp.where(a16 == k, base, zero_b) for k in range(nk)], axis=1)
        both = jnp.dot(hot, rb[...], preferred_element_type=F32)
        r = both[:, :LANES] + both[:, LANES:]
        p_v[at : at + m * LANES, :] = both[:, :LANES].astype(BF16)
        r_out[at : at + m * LANES, :] = r
        rr += fold(r * r)

    fetch.wait()
    for g in range(nblk // m):
        at = g * m * LANES
        p = p_v[at : at + m * LANES, :]
        r = r_out[at : at + m * LANES, :]
        p16 = spread(2, g).astype(BF16)

        def pairs(k0, acc):
            masked = jnp.concatenate(
                [jnp.where(p16 == k0 + k, p, zero_b)
                 for k in range(gp)], axis=1)
            mats = jnp.concatenate(
                [jnp.concatenate([blocks[2 * (k0 + k)], blocks[2 * (k0 + k) + 1]], axis=1)
                 for k in range(gp)], axis=0)
            return acc + jnp.dot(masked, mats, preferred_element_type=F32)

        acc = jnp.zeros((m * LANES, 2 * LANES), F32)
        for k0 in range(0, npair, gp):
            acc = pairs(k0, acc)
        qb = jnp.where(spread(3, g) > 0.5, acc[:, LANES:], acc[:, :LANES]).astype(BF16)
        q_out[at : at + m * LANES, :] = qb
        q = qb.astype(F32)
        pq += fold(r * q)
        qq += fold(q * q)

    def one_copy(slot, k):
        return pltpu.make_async_remote_copy(
            one_buf.at[slot], one_buf.at[slot], one_s.at[k], one_r.at[slot],
            device_id=(sx, lax.rem(sy + k, nsy)), device_id_type=MESH)

    def two_copy(slot, k):
        return pltpu.make_async_remote_copy(
            two_buf.at[slot], two_buf.at[slot], two_s.at[k], two_r.at[slot],
            device_id=(lax.rem(sx + k, nsx), sy), device_id_type=MESH)

    one_buf[sy] = jnp.concatenate([jnp.sum(v, axis=0, keepdims=True) for v in (rr, pq, qq)]
                                  + [jnp.zeros((5, LANES), F32)], axis=0)
    pl.semaphore_wait(barrier, nsx + nsy - 2)
    for k in range(1, nsy):
        one_copy(sy, k).start()
    for a in range(nk // 2):
        at = a * LANES
        cr[at : at + LANES, :] = rim_ref[at : at + LANES, :] * count[:, a : a + 1]
    for k in range(1, nsy):
        one_copy(lax.rem(sy + k, nsy), k).wait_recv()
    two_buf[sx] = jnp.sum(one_buf[...], axis=0)
    for k in range(1, nsx):
        two_copy(sx, k).start()
    for a in range(nk // 2, nk):
        at = a * LANES
        cr[at : at + LANES, :] = rim_ref[at : at + LANES, :] * count[:, a : a + 1]
    for k in range(1, nsx):
        two_copy(lax.rem(sx + k, nsx), k).wait_recv()
    sums_out[...] = jnp.sum(two_buf[...], axis=0)
    for k in range(1, nsy):
        one_copy(sy, k).wait_send()
    for k in range(1, nsx):
        two_copy(sx, k).wait_send()


def back_kernel(sp, cr, r_ref, q_ref, sums, out, res, direc,
                left, right, top, bottom, res_v, dir_v, sem):
    rows, cols = out.shape
    tiles = r_ref.shape[0]
    runs = cols // LANES
    inner = pltpu.make_async_copy(
        sp.at[16 : rows, 2 * LANES : cols],
        out.at[8 : rows - 8, LANES : cols - LANES], sem.at[0])
    inner.start()
    copies = [inner]
    total = jnp.sum(sums[...], axis=1, keepdims=True)
    rr, pq, qq = total[0:1], total[1:2], total[2:3]
    alpha = rr / pq
    beta = (rr - 2.0 * alpha * pq + alpha * alpha * qq) / rr

    nch = 4
    size = tiles // nch
    for k in range(nch):
        sl = slice(k * size, (k + 1) * size)

        @pl.loop(0, size // 64)
        def _(t, k=k):
            at = pl.multiple_of(k * size + t * 64, 64)
            r = r_ref[pl.ds(at, 64), :]
            v = r - alpha * q_ref[pl.ds(at, 64), :].astype(F32)
            res_v[pl.ds(at, 64), :] = v
            dir_v[pl.ds(at, 64), :] = v + beta * r

        for src, dst, i in ((res_v, res, 1 + k), (dir_v, direc, 1 + nch + k)):
            cp = pltpu.make_async_copy(src.at[sl], dst.at[sl], sem.at[i])
            cp.start()
            copies.append(cp)

    @pl.loop(0, rows // 64)
    def _(t):
        at = pl.multiple_of(t * 64, 64)
        left[pl.ds(at, 64), :] = sp[pl.ds(at + 8, 64), LANES : 2 * LANES] + alpha * cr[pl.ds(at, 64), :]
        right[pl.ds(at, 64), :] = (sp[pl.ds(at + 8, 64), cols : cols + LANES]
                                   + alpha * cr[pl.ds(at + rows, 64), :])

    top[...] = sp[8:16, 2 * LANES : cols]
    bottom[...] = sp[rows : rows + 8, 2 * LANES : cols]
    for k in range(1, runs - 1):
        sl = slice((k - 1) * LANES, k * LANES)
        top[0:1, sl] = top[0:1, sl] + alpha * cr[2 * rows + k : 2 * rows + k + 1, :]
        bottom[7:8, sl] = bottom[7:8, sl] + alpha * cr[2 * rows + runs + k : 2 * rows + runs + k + 1, :]
    i = 1 + 2 * nch
    for src, dst in ((left, out.at[:, 0:LANES]), (right, out.at[:, cols - LANES : cols]),
                     (top, out.at[0:8, LANES : cols - LANES]),
                     (bottom, out.at[rows - 8 : rows, LANES : cols - LANES])):
        cp = pltpu.make_async_copy(src, dst, sem.at[i])
        cp.start()
        copies.append(cp)
        i += 1
    for cp in copies:
        cp.wait()


def per_device(nsx, nsy, rhs, sigma, tile_list, tile_owner, schur_blocks):
    rows, cols = rhs.shape
    tiles = tile_list.shape[0]
    nk = -(-(2 * rows + 2 * (cols // LANES)) // LANES)
    vm = pl.BlockSpec(memory_space=pltpu.VMEM)
    hbm = pl.BlockSpec(memory_space=pl.ANY)
    big = pl.BlockSpec(memory_space=pltpu.HBM)
    dma = pltpu.SemaphoreType.DMA
    padded = (rows + 16, cols + 2 * LANES)
    kept = pltpu.VMEM

    def in_hbm(v):
        return pltpu.with_memory_space_constraint(v, pltpu.HBM)

    blocks = lax.all_gather(schur_blocks, ("sx", "sy"), axis=0, tiled=True)
    sp, rim = pl.pallas_call(
        functools.partial(front_kernel, nsx, nsy),
        out_shape=[kept(padded, F32), kept((nk * LANES, LANES), F32)],
        in_specs=[big] * 2,
        out_specs=[vm] * 2,
        scratch_shapes=[
            pltpu.VMEM((rows, cols), F32), pltpu.VMEM((rows, cols), F32), pltpu.VMEM(padded, F32),
            pltpu.VMEM((2, 2, 1, cols), F32), pltpu.VMEM((2, 2, 1, cols), F32),
            pltpu.VMEM((2, 2, 8, LANES), F32), pltpu.VMEM((2, 2, 8, LANES), F32),
            dma((2, 8)), dma((2, 4)), dma((2, 4)),
        ],
        compiler_params=pltpu.CompilerParams(
            collective_id=0, has_side_effects=True, vmem_limit_bytes=32 * 2**20),
        cost_estimate=pl.CostEstimate(flops=40 * rows * cols, bytes_accessed=12 * rows * cols,
                                      transcendentals=0),
        name="front",
    )(in_hbm(rhs), in_hbm(sigma))
    cr, r, q, sums = pl.pallas_call(
        functools.partial(product_kernel, nsx, nsy, rows, cols // LANES),
        out_shape=[kept((nk * LANES, LANES), F32), kept((tiles, LANES), F32), kept((tiles, LANES), BF16),
                   kept((8, LANES), F32)],
        in_specs=[big, big, big, vm],
        out_specs=[vm] * 4,
        scratch_shapes=[pltpu.VMEM((nk * LANES, 2 * LANES), BF16), pltpu.VMEM((tiles, LANES), BF16),
                        pltpu.VMEM((tiles // LANES, LANES), jnp.int32),
                        pltpu.VMEM((tiles // LANES, LANES), jnp.int32),
                        pltpu.VMEM((nsx * nsy, LANES, LANES), BF16),
                        pltpu.VMEM((nsy, 8, LANES), F32), pltpu.VMEM((nsx, 8, LANES), F32), dma((3,)),
                        dma((nsy,)), dma((nsy,)), dma((nsx,)), dma((nsx,))],
        compiler_params=pltpu.CompilerParams(
            collective_id=1, has_side_effects=True, vmem_limit_bytes=24 * 2**20),
        name="products",
    )(in_hbm(tile_list.reshape(-1, LANES)), in_hbm(tile_owner.reshape(-1, LANES)), in_hbm(blocks), rim)
    nch = 4
    return pl.pallas_call(
        back_kernel,
        out_shape=[jax.ShapeDtypeStruct((rows, cols), F32), jax.ShapeDtypeStruct((tiles, LANES), F32),
                   jax.ShapeDtypeStruct((tiles, LANES), F32)],
        in_specs=[vm] * 5,
        out_specs=[hbm] * 3,
        scratch_shapes=[
            pltpu.VMEM((rows, LANES), F32), pltpu.VMEM((rows, LANES), F32),
            pltpu.VMEM((8, cols - 2 * LANES), F32), pltpu.VMEM((8, cols - 2 * LANES), F32),
            pltpu.VMEM((tiles, LANES), F32), pltpu.VMEM((tiles, LANES), F32),
            dma((1 + 2 * nch + 4,)),
        ],
        compiler_params=pltpu.CompilerParams(vmem_limit_bytes=16 * 2**20),
        name="back",
    )(sp, cr, r, q, sums)


def solution(mesh):
    nsx, nsy = mesh.shape["sx"], mesh.shape["sy"]
    in_specs = (
        P("sx", "sy"),
        P("sx", "sy"),
        P(("sx", "sy")),
        P(("sx", "sy"), None),
        P(("sx", "sy"), None, None),
    )
    out_specs = (P("sx", "sy"), P(("sx", "sy"), None), P(("sx", "sy"), None))

    def body(*args):
        return tuple(per_device(nsx, nsy, *args))

    return jax.shard_map(body, mesh=mesh, in_specs=in_specs, out_specs=out_specs, check_vma=False)
```
